512 devices in a mesh: pool: 128 (over z, y, core), pb: 4 (over x).
Axes of the slice: x: 4, y: 8, z: 8, core: 2. Of those that a mesh axis runs over, the one named last changes fastest.
Arguments:
- adjoint_source: float32 [3, 4, 65536], P(None, None, 'pool'), may hold values from -6 to 6
- deviation: float32 [3, 4, 65536], P(None, None, 'pool'), may hold values from -6 to 6
- relax_time: float32 [4, 65536], P(None, 'pool'), may hold values from 0.3 to 3
- band_window: int32 [65536], P('pool'), may hold values from 1 to 15
- pair_src: int32 [524288], P(('pool', 'pb')), may hold values from 0 to 511
- pair_dst: int32 [524288], P(('pool', 'pb')), may hold values from 0 to 511
- bucket_fill: int32 [512, 128], P(('pool', 'pb')), may hold values from 2 to 8, as said below
- coupling: float32 [16, 524288], P(None, ('pool', 'pb')), may hold values from 0.05 to 0.5
Outputs:
- multiplier: float32 [3, 4, 65536], P(None, None, 'pool')
- coupling_grad: float32 [16, 524288], P(None, ('pool', 'pb'))
The draws below stay inside these ranges and needn't reach their ends.
Inputs may be any that keep to these rules, and one draw needn't show every extreme that they name: The first bucket_fill[t, o] slots of the block of 8 slots that device t addresses to pool index o are live, the rest hold no pair. On every device at least one block is full.
All inputs are finite; a program needn't handle non-finite values.
Results may differ from the reference program's by a relative error of at most 0.00002.
Values sent between devices are 32-bit elements; how exact they have to be, the bound alone decides.
No kernel may reach another device: no remote copies, remote signals or barrier semaphores. Data moves between devices by JAX's collectives and lax.ppermute only.
A program may use at most 64 MiB of HBM per device.

```python
import math
import jax
import jax.numpy as jnp

NB = 4
ND = 3
ITERS = 2
S_DEV = 512
ENT_DEV = 1024
CAP = 8
NS = 65536
ENTRIES = 524288
N_PB = 4


def draw_bucket_fill(key, part):
    key = jax.random.fold_in(key, 7)
    first, second = jax.random.split(key)
    devs = ENTRIES // ENT_DEV
    pools = NS // S_DEV
    shares = jax.random.randint(first, (devs, pools), max(1, CAP // 4), CAP // 2 + 1)
    heated = jax.random.randint(second, (pools,), 0, 4) == 0
    home = jnp.arange(devs, dtype=jnp.int32) // (devs // pools)
    forced = jnp.arange(pools, dtype=jnp.int32)[None, :] == ((home + 1) % pools)[:, None]
    return jnp.where(heated[None, :] | forced, CAP, shares).astype(jnp.int32)


def touch_ends(values, stream_key, smallest, high):
    shape = values.shape
    spot = [jax.random.randint(jax.random.fold_in(stream_key, axis), (), 0, shape[axis]) for axis in range(len(shape))]
    values = values.at[tuple(spot)].set(smallest)
    longest = shape.index(max(shape))
    spot[longest] = (spot[longest] + 1) % shape[longest]
    return values.at[tuple(spot)].set(high)


def block_levels(own_key, dims, cuts, low, high):
    def one(position, parts):
        steps = jax.random.uniform(jax.random.fold_in(jax.random.fold_in(own_key, 6), position), (parts,), jnp.float32, low / len(cuts), high / len(cuts))
        return jnp.repeat(jnp.exp(steps), dims[position] // parts).reshape((-1,) + (1,) * (len(dims) - position - 1))

    level = one(*cuts[0])
    for cut in cuts[1:]:
        level = level * one(*cut)
    return level


def normal_values(key, shape, spread, limit, cuts=(), held_as=jnp.bfloat16):
    array = spread * jax.random.normal(key, shape, jnp.float32)
    if cuts:
        array = array * block_levels(key, shape, cuts, -0.22, 0.18)
    return jnp.clip(array, -limit, limit).astype(held_as)


def setup_inputs(seed: int = 0) -> dict:
    keys = jax.random.split(jax.random.key(seed), 9)
    return {
        "adjoint_source": normal_values(keys[0], (ND, NB, NS), 1.0, 6.0, ((2, 128),), jnp.float32),
        "deviation": normal_values(keys[1], (ND, NB, NS), 1.0, 6.0, ((2, 128),), jnp.float32),
        "relax_time": jnp.clip(jnp.exp(math.log(3.0) - 2.3025851 * jax.random.uniform(keys[2], (NB, NS), jnp.float32) ** block_levels(keys[2], (NB, NS), ((1, 128),), -0.2, 0.2)), 0.3, 3.0),
        "band_window": touch_ends(jax.random.randint(keys[3], (NS,), 1, 16), jax.random.fold_in(keys[3], 1), 1, 15).astype(jnp.int32),
        "pair_src": touch_ends(jax.random.randint(keys[4], (ENTRIES,), 0, S_DEV), jax.random.fold_in(keys[4], 1), 0, S_DEV - 1).astype(jnp.int32),
        "pair_dst": touch_ends(jax.random.randint(keys[5], (ENTRIES,), 0, S_DEV), jax.random.fold_in(keys[5], 1), 0, S_DEV - 1).astype(jnp.int32),
        "bucket_fill": draw_bucket_fill(jax.random.fold_in(keys[8], 71), 0),
        "coupling": jnp.clip(jnp.exp(math.log(0.5) - 2.3025851 * jax.random.uniform(keys[7], (NB * NB, ENTRIES), jnp.float32) ** block_levels(keys[7], (NB * NB, ENTRIES), ((1, 512),), -0.2, 0.2)), 0.05, 0.5),
    }


def reference(adjoint_source, deviation, relax_time, band_window, pair_src, pair_dst, bucket_fill, coupling):
    total = pair_src.shape[0]
    slots = jnp.arange(total, dtype=jnp.int32)
    device = slots // ENT_DEV
    local_slot = slots % ENT_DEV
    owner = local_slot // CAP
    live = ((local_slot % CAP) < bucket_fill[device, owner]).astype(jnp.float32)
    kstate = ((device // N_PB) * S_DEV + pair_src).astype(jnp.int32)
    qstate = (owner * S_DEV + pair_dst).astype(jnp.int32)
    bands = jnp.arange(NB, dtype=jnp.int32)
    window = ((band_window[None, :] >> bands[:, None]) & 1).astype(jnp.float32)
    source = window[None] * adjoint_source
    couple = coupling.reshape(NB, NB, total)
    multiplier = source
    for step in range(ITERS):
        moment = multiplier * relax_time[None]
        picked = jnp.take(moment, kstate, axis=2)
        terms = couple[0][None] * picked[:, 0][:, None]
        for band in range(1, NB):
            terms = terms + couple[band][None] * picked[:, band][:, None]
        terms = terms * live
        incoming = jnp.zeros((ND, NB, NS), jnp.float32).at[:, :, qstate].add(terms)
        multiplier = source + window[None] * incoming
    moment = multiplier * relax_time[None]
    picked = jnp.take(moment, kstate, axis=2)
    farther = jnp.take(window[None] * deviation, qstate, axis=2)
    grads = picked[0][:, None] * farther[0][None]
    for direction in range(1, ND):
        grads = grads + picked[direction][:, None] * farther[direction][None]
    grads = grads * live
    return multiplier, grads.reshape(NB * NB, total)
```

```python
import functools

import jax
import jax.numpy as jnp
from jax import lax
from jax.experimental import pallas as pl
from jax.experimental.pallas import tpu as pltpu
from jax.sharding import PartitionSpec as P

ITERS = 2
WIDTH = 16
F32 = jnp.float32
BF16 = jnp.bfloat16
MIB = 1024 * 1024


def split3(x):
    high = x.astype(BF16)
    rest = x - high.astype(F32)
    middle = rest.astype(BF16)
    low = (rest - middle.astype(F32)).astype(BF16)
    return jnp.concatenate([high, middle, low], axis=0)


def tiles_of(x):
    parts = split3(x)
    width = min(128, x.shape[1])
    return jnp.concatenate([parts[:, t : t + width] for t in range(0, x.shape[1], width)], axis=0)


def whole(parts):
    return parts[:16] + parts[16:32] + parts[32:48]


def select(x, index):
    width = min(128, x.shape[1])
    rows = lax.broadcasted_iota(jnp.int32, (width, index.shape[1]), 0)
    hot = jnp.where(rows == (index & (width - 1)), 1.0, 0.0).astype(BF16)
    found = jnp.dot(tiles_of(x), hot, preferred_element_type=F32)
    at = jnp.broadcast_to(index, (16, index.shape[1])) >> (width.bit_length() - 1)
    total = whole(found[:48])
    for tile in range(1, x.shape[1] // width):
        total = jnp.where(at == tile, whole(found[48 * tile : 48 * tile + 48]), total)
    return total


def pick(x, index):
    parts = []
    width = min(128, index.shape[1])
    for first in range(0, index.shape[1], width):
        at = jnp.broadcast_to(index[:, first : first + width], (x.shape[0], width))
        part = jnp.zeros(at.shape, F32)
        for tile in range(x.shape[1] // 128):
            columns = x[:, 128 * tile : 128 * (tile + 1)]
            found = jnp.take_along_axis(columns, at & 127, axis=1, mode="promise_in_bounds")
            part = jnp.where(at >> 7 == tile, found, part)
        parts.append(part)
    return jnp.concatenate(parts, axis=1)


def rows16(ref):
    return jnp.concatenate([ref[0], ref[1], ref[2], jnp.zeros_like(ref[0])], axis=0)


def window16(window_ref):
    rows = lax.broadcasted_iota(jnp.int32, (16, window_ref.shape[1]), 0)
    return ((window_ref[...] >> (rows & 3)) & 1).astype(F32)


def live_row(fill_ref, slots):
    owners = fill_ref.shape[1]
    capacity = slots // owners
    fill = jnp.broadcast_to(fill_ref[...].astype(F32), (8, owners))
    lane = lax.broadcasted_iota(jnp.int32, (8, owners), 1)
    place = (lane & (capacity - 1)).astype(F32)
    parts = []
    for first in range(0, owners, owners // capacity):
        filled = jnp.take_along_axis(fill, first + (lane >> (capacity.bit_length() - 1)), axis=1, mode="promise_in_bounds")
        parts.append(jnp.where(place < filled, 1.0, 0.0)[:1])
    return jnp.concatenate(parts, axis=1)


def repeat_rows(x, first, step, count):
    row = lax.broadcasted_iota(jnp.int32, (16, x.shape[1]), 0)
    out = jnp.broadcast_to(x[first : first + 1], row.shape)
    for i in range(1, count):
        out = jnp.where(row >= 4 * i, x[first + step * i : first + step * i + 1], out)
    return out


def scatter_terms(picked, live, couple):
    total = None
    for band in range(4):
        block = couple[4 * band : 4 * band + 4]
        block = jnp.concatenate([block, block, block, jnp.zeros_like(block)], axis=0)
        term = block * repeat_rows(picked, band, 4, 3)
        total = term if total is None else total + term
    return total * live


def slots_to_rows(x, flat_ref):
    owners = x.shape[1] // 8
    flat_ref[...] = x.T
    return jnp.concatenate([flat_ref[pl.ds(j, owners, stride=8), :] for j in range(8)], axis=1)


def pack(x):
    half = x.shape[1] // 2
    tail = jnp.concatenate([x[8:12, :half], x[8:12, half:]], axis=0)
    return jnp.concatenate([x[:8], tail], axis=1)


def unpack(x):
    whole = x.shape[1] * 2 // 3
    tail = jnp.concatenate([x[:4, whole:], x[4:, whole:]], axis=1)
    return jnp.concatenate([x[:8, :whole], jnp.concatenate([tail, jnp.zeros_like(tail)], axis=0)], axis=0)


def received_slots(rows):
    turned = rows.T
    return jnp.concatenate([turned[WIDTH * j : WIDTH * (j + 1)] for j in range(8)], axis=1)


def sums_of(slots, rows, states):
    turned = rows.T.astype(jnp.int32)
    index = jnp.concatenate([turned[WIDTH * j + 12 : WIDTH * j + 13] for j in range(8)], axis=1)
    state = lax.broadcasted_iota(jnp.int32, (states, index.shape[1]), 0)
    hot = jnp.where(state == index, 1.0, 0.0).astype(BF16)
    both = (((1,), (1,)), ((), ()))
    return whole(lax.dot_general(split3(slots), hot, both, preferred_element_type=F32))


def zero_kernel(out_ref):
    out_ref[...] = jnp.zeros_like(out_ref)


def first_kernel(
    zero_ref, couple_ref, source_ref, relax_ref, window_ref, src_ref, dst_ref, fill_ref, out_ref, flat_ref
):
    live = live_row(fill_ref, src_ref.shape[1])
    relax = jnp.concatenate([relax_ref[...]] * 4, axis=0)
    moment = rows16(source_ref) * window16(window_ref) * relax
    terms = scatter_terms(pick(moment, src_ref[...]), live, couple_ref[...])
    row = lax.broadcasted_iota(jnp.int32, terms.shape, 0)
    terms = jnp.where(row == 12, dst_ref[...].astype(F32) + zero_ref[:1, :1], terms)
    out_ref[...] = slots_to_rows(terms, flat_ref)


def gather_kernel(rows_ref, index_ref, out_ref, *, states):
    senders = index_ref.shape[0]
    depth = rows_ref.shape[0] // senders
    rows = rows_ref[...] if depth == 1 else rows_ref[pl.ds(0, senders, stride=depth), :]
    packed = pack(sums_of(received_slots(rows), index_ref[...], states))
    for i in range(out_ref.shape[0]):
        out_ref[i] = packed


def returned_rows(dev_ref, window_ref, index_ref):
    masked = rows16(dev_ref) * window16(window_ref)
    turned = index_ref[...].T.astype(jnp.int32)
    found = [pick(masked, turned[WIDTH * j + 12 : WIDTH * j + 13]) for j in range(8)]
    return jnp.concatenate(found, axis=0).T


def multiplier_of(part, source_ref, window_ref):
    window = window16(window_ref)
    return window * (rows16(source_ref) + unpack((part[0] + part[1]) + (part[2] + part[3])))


def second_kernel(
    parts_ref, index_ref, dev_ref, source_ref, relax_ref, window_ref, src_ref, fill_ref, couple_ref, out_ref, flat_ref
):
    senders = index_ref.shape[0]
    out_ref[pl.ds(1, senders, stride=2), :] = returned_rows(dev_ref, window_ref, index_ref)
    relax = jnp.concatenate([relax_ref[...]] * 4, axis=0)
    moment = relax * multiplier_of(parts_ref, source_ref, window_ref)
    live = live_row(fill_ref, src_ref.shape[1])
    terms = scatter_terms(select(moment, src_ref[...]), live, couple_ref[...])
    out_ref[pl.ds(0, senders, stride=2), :] = slots_to_rows(terms, flat_ref)


def last_kernel(
    parts_ref, rows_ref, source_ref, relax_ref, window_ref, src_ref, fill_ref, multiplier_ref, grad_ref, flat_ref
):
    owners = rows_ref.shape[0] // 2
    rows = rows_ref[pl.ds(1, owners, stride=2), :]
    for j in range(8):
        flat_ref[pl.ds(j, owners, stride=8), :] = rows[:, WIDTH * j : WIDTH * (j + 1)]
    fetched = flat_ref[...].T
    relax = jnp.concatenate([relax_ref[...]] * 4, axis=0)
    multiplier = multiplier_of(parts_ref, source_ref, window_ref)
    for d in range(3):
        multiplier_ref[d] = multiplier[4 * d : 4 * d + 4]
    picked = select(relax * multiplier, src_ref[...])
    total = None
    for d in range(3):
        far = fetched[4 * d : 4 * d + 4]
        term = repeat_rows(picked, 4 * d, 1, 4) * jnp.concatenate([far] * 4, axis=0)
        total = term if total is None else total + term
    grad_ref[...] = total * live_row(fill_ref, src_ref.shape[1])


def call(kernel, out_shape, scratch, *operands, cost=None):
    return pl.pallas_call(
        kernel,
        out_shape=out_shape,
        in_specs=[pl.BlockSpec(memory_space=pltpu.VMEM)] * len(operands),
        scratch_shapes=scratch,
        compiler_params=pltpu.CompilerParams(vmem_limit_bytes=24 * MIB),
        cost_estimate=cost,
    )(*operands)


def exchange(rows):
    pools = lax.axis_size("pool")
    x = rows.reshape(pools, -1, 128)
    return lax.all_to_all(x, "pool", 0, 0, tiled=True).reshape(rows.shape)


def share(part):
    return lax.all_to_all(part, "pb", 0, 0, tiled=True)


def local(
    adjoint_source, deviation, relax_time, band_window, pair_src, pair_dst, bucket_fill, coupling
):
    states = band_window.shape[0]
    slots = pair_src.shape[0]
    pools = lax.axis_size("pool")
    window = band_window.reshape(1, states)
    src = pair_src.reshape(1, slots)
    dst = pair_dst.reshape(1, slots)
    sds = jax.ShapeDtypeStruct
    flat = pltpu.VMEM((slots, WIDTH), F32)
    partial = sds((lax.axis_size("pb"), 8, states * 3 // 2), F32)

    cost = pl.CostEstimate(flops=10**10, bytes_accessed=0, transcendentals=0)
    zero = call(zero_kernel, sds((8, 128), F32), [], cost=cost)
    sent = call(
        first_kernel, sds((pools, 128), F32), [flat],
        zero, coupling, adjoint_source, relax_time, window, src, dst, bucket_fill,
    )
    index = exchange(sent)
    gather = functools.partial(gather_kernel, states=states)
    parts = share(call(gather, partial, [], index, index))
    sent = call(
        second_kernel, sds((2 * pools, 128), F32), [flat],
        parts, index, deviation, adjoint_source, relax_time, window, src, bucket_fill, coupling,
    )
    rows = exchange(sent)
    parts = share(call(gather, partial, [], rows, index))
    return call(
        last_kernel, (sds(adjoint_source.shape, F32), sds(coupling.shape, F32)), [flat],
        parts, rows, adjoint_source, relax_time, window, src, bucket_fill,
    )


def solution(mesh):
    in_specs = (
        P(None, None, "pool"),
        P(None, None, "pool"),
        P(None, "pool"),
        P("pool"),
        P(("pool", "pb")),
        P(("pool", "pb")),
        P(("pool", "pb"), None),
        P(None, ("pool", "pb")),
    )
    out_specs = (P(None, None, "pool"), P(None, ("pool", "pb")))
    return jax.shard_map(local, mesh=mesh, in_specs=in_specs, out_specs=out_specs, check_vma=False)
```

```python
import functools

import jax
import jax.numpy as jnp
from jax import lax
from jax.experimental import pallas as pl
from jax.experimental.pallas import tpu as pltpu
from jax.sharding import PartitionSpec as P

ITERS = 2
WIDTH = 16
F32 = jnp.float32
BF16 = jnp.bfloat16
MIB = 1024 * 1024


def split3(x):
    high = x.astype(BF16)
    rest = x - high.astype(F32)
    middle = rest.astype(BF16)
    low = (rest - middle.astype(F32)).astype(BF16)
    return jnp.concatenate([high, middle, low], axis=0)


def tiles_of(x):
    parts = split3(x)
    width = min(128, x.shape[1])
    return jnp.concatenate([parts[:, t : t + width] for t in range(0, x.shape[1], width)], axis=0)


def whole(parts):
    return parts[:16] + parts[16:32] + parts[32:48]


def select(x, index):
    width = min(128, x.shape[1])
    rows = lax.broadcasted_iota(jnp.int32, (width, index.shape[1]), 0)
    hot = jnp.where(rows == (index & (width - 1)), 1.0, 0.0).astype(BF16)
    found = jnp.dot(tiles_of(x), hot, preferred_element_type=F32)
    at = jnp.broadcast_to(index, (16, index.shape[1])) >> (width.bit_length() - 1)
    total = whole(found[:48])
    for tile in range(1, x.shape[1] // width):
        total = jnp.where(at == tile, whole(found[48 * tile : 48 * tile + 48]), total)
    return total


def pick(x, index):
    parts = []
    width = min(128, index.shape[1])
    for first in range(0, index.shape[1], width):
        at = jnp.broadcast_to(index[:, first : first + width], (x.shape[0], width))
        part = jnp.zeros(at.shape, F32)
        for tile in range(x.shape[1] // 128):
            columns = x[:, 128 * tile : 128 * (tile + 1)]
            found = jnp.take_along_axis(columns, at & 127, axis=1, mode="promise_in_bounds")
            part = jnp.where(at >> 7 == tile, found, part)
        parts.append(part)
    return jnp.concatenate(parts, axis=1)


def rows16(ref):
    return jnp.concatenate([ref[0], ref[1], ref[2], jnp.zeros_like(ref[0])], axis=0)


def window16(window_ref):
    rows = lax.broadcasted_iota(jnp.int32, (16, window_ref.shape[1]), 0)
    return ((window_ref[...] >> (rows & 3)) & 1).astype(F32)


def live_row(fill_ref, slots):
    owners = fill_ref.shape[1]
    capacity = slots // owners
    fill = jnp.broadcast_to(fill_ref[...].astype(F32), (8, owners))
    lane = lax.broadcasted_iota(jnp.int32, (8, owners), 1)
    place = (lane & (capacity - 1)).astype(F32)
    parts = []
    for first in range(0, owners, owners // capacity):
        filled = jnp.take_along_axis(fill, first + (lane >> (capacity.bit_length() - 1)), axis=1, mode="promise_in_bounds")
        parts.append(jnp.where(place < filled, 1.0, 0.0)[:1])
    return jnp.concatenate(parts, axis=1)


def repeat_rows(x, first, step, count):
    row = lax.broadcasted_iota(jnp.int32, (16, x.shape[1]), 0)
    out = jnp.broadcast_to(x[first : first + 1], row.shape)
    for i in range(1, count):
        out = jnp.where(row >= 4 * i, x[first + step * i : first + step * i + 1], out)
    return out


def scatter_terms(picked, live, couple):
    total = None
    for band in range(4):
        block = couple[4 * band : 4 * band + 4]
        block = jnp.concatenate([block, block, block, jnp.zeros_like(block)], axis=0)
        term = block * repeat_rows(picked, band, 4, 3)
        total = term if total is None else total + term
    return total * live


def slots_to_rows(x, flat_ref):
    owners = x.shape[1] // 8
    flat_ref[...] = x.T
    return jnp.concatenate([flat_ref[pl.ds(j, owners, stride=8), :] for j in range(8)], axis=1)


def pack(x):
    half = x.shape[1] // 2
    tail = jnp.concatenate([x[8:12, :half], x[8:12, half:]], axis=0)
    return jnp.concatenate([x[:8], tail], axis=1)


def unpack(x):
    whole = x.shape[1] * 2 // 3
    tail = jnp.concatenate([x[:4, whole:], x[4:, whole:]], axis=1)
    return jnp.concatenate([x[:8, :whole], jnp.concatenate([tail, jnp.zeros_like(tail)], axis=0)], axis=0)


def received_slots(rows):
    turned = rows.T
    return jnp.concatenate([turned[WIDTH * j : WIDTH * (j + 1)] for j in range(8)], axis=1)


def hot_lanes(index, count):
    lanes = lax.broadcasted_iota(jnp.int32, (index.shape[0], count), 1)
    return jnp.where(lanes == index, 1.0, 0.0).astype(BF16)


def received_hot(rows, count):
    index = rows.astype(jnp.int32)
    return jnp.concatenate(
        [hot_lanes(index[:, WIDTH * j + 12 : WIDTH * j + 13], count) for j in range(8)], axis=0
    )


def zero_kernel(out_ref):
    out_ref[...] = jnp.zeros_like(out_ref)


def first_kernel(
    zero_ref, couple_ref, source_ref, relax_ref, window_ref, src_ref, dst_ref, fill_ref, out_ref, flat_ref
):
    live = live_row(fill_ref, src_ref.shape[1])
    relax = jnp.concatenate([relax_ref[...]] * 4, axis=0)
    moment = rows16(source_ref) * window16(window_ref) * relax
    terms = scatter_terms(pick(moment, src_ref[...]), live, couple_ref[...])
    row = lax.broadcasted_iota(jnp.int32, terms.shape, 0)
    terms = jnp.where(row == 12, dst_ref[...].astype(F32) + zero_ref[:1, :1], terms)
    out_ref[...] = slots_to_rows(terms, flat_ref)


def gather_kernel(rows_ref, index_ref, out_ref, *, states):
    senders = index_ref.shape[0]
    depth = rows_ref.shape[0] // senders
    rows = rows_ref[...] if depth == 1 else rows_ref[pl.ds(0, senders, stride=depth), :]
    hot = received_hot(index_ref[...], states)
    packed = pack(whole(jnp.dot(split3(received_slots(rows)), hot, preferred_element_type=F32)))
    for i in range(out_ref.shape[0]):
        out_ref[i] = packed


def returned_rows(dev_ref, window_ref, index_ref):
    masked = rows16(dev_ref) * window16(window_ref)
    turned = index_ref[...].T.astype(jnp.int32)
    found = [pick(masked, turned[WIDTH * j + 12 : WIDTH * j + 13]) for j in range(8)]
    return jnp.concatenate(found, axis=0).T


def multiplier_of(part, source_ref, window_ref):
    window = window16(window_ref)
    return window * (rows16(source_ref) + unpack((part[0] + part[1]) + (part[2] + part[3])))


def second_kernel(
    parts_ref, index_ref, dev_ref, source_ref, relax_ref, window_ref, src_ref, fill_ref, couple_ref, out_ref, flat_ref
):
    senders = index_ref.shape[0]
    out_ref[pl.ds(1, senders, stride=2), :] = returned_rows(dev_ref, window_ref, index_ref)
    relax = jnp.concatenate([relax_ref[...]] * 4, axis=0)
    moment = relax * multiplier_of(parts_ref, source_ref, window_ref)
    live = live_row(fill_ref, src_ref.shape[1])
    terms = scatter_terms(select(moment, src_ref[...]), live, couple_ref[...])
    out_ref[pl.ds(0, senders, stride=2), :] = slots_to_rows(terms, flat_ref)


def last_kernel(
    parts_ref, rows_ref, source_ref, relax_ref, window_ref, src_ref, fill_ref, multiplier_ref, grad_ref, flat_ref
):
    owners = rows_ref.shape[0] // 2
    rows = rows_ref[pl.ds(1, owners, stride=2), :]
    for j in range(8):
        flat_ref[pl.ds(j, owners, stride=8), :] = rows[:, WIDTH * j : WIDTH * (j + 1)]
    fetched = flat_ref[...].T
    relax = jnp.concatenate([relax_ref[...]] * 4, axis=0)
    multiplier = multiplier_of(parts_ref, source_ref, window_ref)
    for d in range(3):
        multiplier_ref[d] = multiplier[4 * d : 4 * d + 4]
    picked = select(relax * multiplier, src_ref[...])
    total = None
    for d in range(3):
        far = fetched[4 * d : 4 * d + 4]
        term = repeat_rows(picked, 4 * d, 1, 4) * jnp.concatenate([far] * 4, axis=0)
        total = term if total is None else total + term
    grad_ref[...] = total * live_row(fill_ref, src_ref.shape[1])


def call(kernel, out_shape, scratch, *operands, cost=None):
    return pl.pallas_call(
        kernel,
        out_shape=out_shape,
        in_specs=[pl.BlockSpec(memory_space=pltpu.VMEM)] * len(operands),
        scratch_shapes=scratch,
        compiler_params=pltpu.CompilerParams(vmem_limit_bytes=24 * MIB),
        cost_estimate=cost,
    )(*operands)


def exchange(rows):
    pools = lax.axis_size("pool")
    x = rows.reshape(pools, -1, 128)
    return lax.all_to_all(x, "pool", 0, 0, tiled=True).reshape(rows.shape)


def share(part):
    groups = lax.axis_size("pb")
    orders = [list(range(groups)), [0, *range(groups - 1, 0, -1)]]
    members = [[groups * pool + x for x in orders[pool % 2]] for pool in range(lax.axis_size("pool"))]
    return lax.all_to_all(part, ("pool", "pb"), 0, 0, axis_index_groups=members, tiled=True)


def local(
    adjoint_source, deviation, relax_time, band_window, pair_src, pair_dst, bucket_fill, coupling
):
    states = band_window.shape[0]
    slots = pair_src.shape[0]
    pools = lax.axis_size("pool")
    window = band_window.reshape(1, states)
    src = pair_src.reshape(1, slots)
    dst = pair_dst.reshape(1, slots)
    sds = jax.ShapeDtypeStruct
    flat = pltpu.VMEM((slots, WIDTH), F32)
    partial = sds((lax.axis_size("pb"), 8, states * 3 // 2), F32)

    cost = pl.CostEstimate(flops=10**10, bytes_accessed=0, transcendentals=0)
    zero = call(zero_kernel, sds((8, 128), F32), [], cost=cost)
    sent = call(
        first_kernel, sds((pools, 128), F32), [flat],
        zero, coupling, adjoint_source, relax_time, window, src, dst, bucket_fill,
    )
    index = exchange(sent)
    gather = functools.partial(gather_kernel, states=states)
    parts = share(call(gather, partial, [], index, index))
    sent = call(
        second_kernel, sds((2 * pools, 128), F32), [flat],
        parts, index, deviation, adjoint_source, relax_time, window, src, bucket_fill, coupling,
    )
    rows = exchange(sent)
    parts = share(call(gather, partial, [], rows, index))
    return call(
        last_kernel, (sds(adjoint_source.shape, F32), sds(coupling.shape, F32)), [flat],
        parts, rows, adjoint_source, relax_time, window, src, bucket_fill,
    )


def solution(mesh):
    in_specs = (
        P(None, None, "pool"),
        P(None, None, "pool"),
        P(None, "pool"),
        P("pool"),
        P(("pool", "pb")),
        P(("pool", "pb")),
        P(("pool", "pb"), None),
        P(None, ("pool", "pb")),
    )
    out_specs = (P(None, None, "pool"), P(None, ("pool", "pb")))
    return jax.shard_map(local, mesh=mesh, in_specs=in_specs, out_specs=out_specs, check_vma=False)
```

```python
import functools

import jax
import jax.numpy as jnp
from jax import lax
from jax.experimental import pallas as pl
from jax.experimental.pallas import tpu as pltpu
from jax.sharding import PartitionSpec as P

ITERS = 2
WIDTH = 16
F32 = jnp.float32
BF16 = jnp.bfloat16
MIB = 1024 * 1024


def split3(x):
    high = x.astype(BF16)
    rest = x - high.astype(F32)
    middle = rest.astype(BF16)
    low = (rest - middle.astype(F32)).astype(BF16)
    return jnp.concatenate([high, middle, low], axis=0)


def tiles_of(x):
    parts = split3(x)
    width = min(128, x.shape[1])
    return jnp.concatenate([parts[:, t : t + width] for t in range(0, x.shape[1], width)], axis=0)


def whole(parts):
    return parts[:16] + parts[16:32] + parts[32:48]


def select(x, index):
    width = min(128, x.shape[1])
    rows = lax.broadcasted_iota(jnp.int32, (width, index.shape[1]), 0)
    hot = jnp.where(rows == (index & (width - 1)), 1.0, 0.0).astype(BF16)
    found = jnp.dot(tiles_of(x), hot, preferred_element_type=F32)
    at = jnp.broadcast_to(index, (16, index.shape[1])) >> (width.bit_length() - 1)
    total = whole(found[:48])
    for tile in range(1, x.shape[1] // width):
        total = jnp.where(at == tile, whole(found[48 * tile : 48 * tile + 48]), total)
    return total


def pick(x, index):
    parts = []
    width = min(128, index.shape[1])
    for first in range(0, index.shape[1], width):
        at = jnp.broadcast_to(index[:, first : first + width], (x.shape[0], width))
        part = jnp.zeros(at.shape, F32)
        for tile in range(x.shape[1] // 128):
            columns = x[:, 128 * tile : 128 * (tile + 1)]
            found = jnp.take_along_axis(columns, at & 127, axis=1, mode="promise_in_bounds")
            part = jnp.where(at >> 7 == tile, found, part)
        parts.append(part)
    return jnp.concatenate(parts, axis=1)


def rows16(ref):
    return jnp.concatenate([ref[0], ref[1], ref[2], jnp.zeros_like(ref[0])], axis=0)


def window16(window_ref):
    rows = lax.broadcasted_iota(jnp.int32, (16, window_ref.shape[1]), 0)
    return ((window_ref[...] >> (rows & 3)) & 1).astype(F32)


def live_row(fill_ref, slots):
    owners = fill_ref.shape[1]
    capacity = slots // owners
    fill = jnp.broadcast_to(fill_ref[...].astype(F32), (8, owners))
    lane = lax.broadcasted_iota(jnp.int32, (8, owners), 1)
    place = (lane & (capacity - 1)).astype(F32)
    parts = []
    for first in range(0, owners, owners // capacity):
        filled = jnp.take_along_axis(fill, first + (lane >> (capacity.bit_length() - 1)), axis=1, mode="promise_in_bounds")
        parts.append(jnp.where(place < filled, 1.0, 0.0)[:1])
    return jnp.concatenate(parts, axis=1)


def repeat_rows(x, first, step, count):
    row = lax.broadcasted_iota(jnp.int32, (16, x.shape[1]), 0)
    out = jnp.broadcast_to(x[first : first + 1], row.shape)
    for i in range(1, count):
        out = jnp.where(row >= 4 * i, x[first + step * i : first + step * i + 1], out)
    return out


def scatter_terms(picked, live, couple):
    total = None
    for band in range(4):
        block = couple[4 * band : 4 * band + 4]
        block = jnp.concatenate([block, block, block, jnp.zeros_like(block)], axis=0)
        term = block * repeat_rows(picked, band, 4, 3)
        total = term if total is None else total + term
    return total * live


def slots_to_rows(x, flat_ref):
    owners = x.shape[1] // 8
    flat_ref[...] = x.T
    return jnp.concatenate([flat_ref[pl.ds(j, owners, stride=8), :] for j in range(8)], axis=1)


def pack(x):
    half = x.shape[1] // 2
    tail = jnp.concatenate([x[8:12, :half], x[8:12, half:]], axis=0)
    return jnp.concatenate([x[:8], tail], axis=1)


def unpack(x):
    whole = x.shape[1] * 2 // 3
    tail = jnp.concatenate([x[:4, whole:], x[4:, whole:]], axis=1)
    return jnp.concatenate([x[:8, :whole], jnp.concatenate([tail, jnp.zeros_like(tail)], axis=0)], axis=0)


def received_slots(rows):
    turned = rows.T
    return jnp.concatenate([turned[WIDTH * j : WIDTH * (j + 1)] for j in range(8)], axis=1)


def received_hot(rows, states):
    width = min(256, states)
    lane = lax.broadcasted_iota(jnp.int32, (rows.shape[0], width), 1).astype(F32).astype(BF16)
    blocks = []
    for j in range(8):
        column = rows[:, WIDTH * j + 12 : WIDTH * j + 13]
        parts = [
            jnp.where((column - first).astype(BF16) == lane, jnp.ones_like(lane), jnp.zeros_like(lane))
            for first in range(0, states, width)
        ]
        blocks.append(jnp.concatenate(parts, axis=1))
    return jnp.concatenate(blocks, axis=0)


def zero_kernel(out_ref):
    out_ref[...] = jnp.zeros_like(out_ref)


def first_kernel(
    zero_ref, couple_ref, source_ref, relax_ref, window_ref, src_ref, dst_ref, fill_ref, out_ref, flat_ref
):
    live = live_row(fill_ref, src_ref.shape[1])
    relax = jnp.concatenate([relax_ref[...]] * 4, axis=0)
    moment = rows16(source_ref) * window16(window_ref) * relax
    terms = scatter_terms(pick(moment, src_ref[...]), live, couple_ref[...])
    row = lax.broadcasted_iota(jnp.int32, terms.shape, 0)
    terms = jnp.where(row == 12, dst_ref[...].astype(F32) + zero_ref[:1, :1], terms)
    out_ref[...] = slots_to_rows(terms, flat_ref)


def gather_kernel(rows_ref, index_ref, out_ref, *, states):
    senders = index_ref.shape[0]
    depth = rows_ref.shape[0] // senders
    rows = rows_ref[...] if depth == 1 else rows_ref[pl.ds(0, senders, stride=depth), :]
    hot = received_hot(index_ref[...], states)
    packed = pack(whole(jnp.dot(split3(received_slots(rows)), hot, preferred_element_type=F32)))
    for i in range(out_ref.shape[0]):
        out_ref[i] = packed


def returned_rows(dev_ref, window_ref, index_ref):
    masked = rows16(dev_ref) * window16(window_ref)
    turned = index_ref[...].T.astype(jnp.int32)
    found = [pick(masked, turned[WIDTH * j + 12 : WIDTH * j + 13]) for j in range(8)]
    return jnp.concatenate(found, axis=0).T


def multiplier_of(part, source_ref, window_ref):
    window = window16(window_ref)
    return window * (rows16(source_ref) + unpack((part[0] + part[1]) + (part[2] + part[3])))


def second_kernel(
    parts_ref, index_ref, dev_ref, source_ref, relax_ref, window_ref, src_ref, fill_ref, couple_ref, out_ref, flat_ref
):
    senders = index_ref.shape[0]
    out_ref[pl.ds(1, senders, stride=2), :] = returned_rows(dev_ref, window_ref, index_ref)
    relax = jnp.concatenate([relax_ref[...]] * 4, axis=0)
    moment = relax * multiplier_of(parts_ref, source_ref, window_ref)
    live = live_row(fill_ref, src_ref.shape[1])
    terms = scatter_terms(select(moment, src_ref[...]), live, couple_ref[...])
    out_ref[pl.ds(0, senders, stride=2), :] = slots_to_rows(terms, flat_ref)


def last_kernel(
    parts_ref, rows_ref, source_ref, relax_ref, window_ref, src_ref, fill_ref, multiplier_ref, grad_ref, flat_ref
):
    owners = rows_ref.shape[0] // 2
    rows = rows_ref[pl.ds(1, owners, stride=2), :]
    for j in range(8):
        flat_ref[pl.ds(j, owners, stride=8), :] = rows[:, WIDTH * j : WIDTH * (j + 1)]
    fetched = flat_ref[...].T
    relax = jnp.concatenate([relax_ref[...]] * 4, axis=0)
    multiplier = multiplier_of(parts_ref, source_ref, window_ref)
    for d in range(3):
        multiplier_ref[d] = multiplier[4 * d : 4 * d + 4]
    picked = select(relax * multiplier, src_ref[...])
    total = None
    for d in range(3):
        far = fetched[4 * d : 4 * d + 4]
        term = repeat_rows(picked, 4 * d, 1, 4) * jnp.concatenate([far] * 4, axis=0)
        total = term if total is None else total + term
    grad_ref[...] = total * live_row(fill_ref, src_ref.shape[1])


def call(kernel, out_shape, scratch, *operands, cost=None):
    return pl.pallas_call(
        kernel,
        out_shape=out_shape,
        in_specs=[pl.BlockSpec(memory_space=pltpu.VMEM)] * len(operands),
        scratch_shapes=scratch,
        compiler_params=pltpu.CompilerParams(vmem_limit_bytes=24 * MIB),
        cost_estimate=cost,
    )(*operands)


def exchange(rows):
    pools = lax.axis_size("pool")
    x = rows.reshape(pools, -1, 128)
    return lax.all_to_all(x, "pool", 0, 0, tiled=True).reshape(rows.shape)


def share(part):
    return lax.all_to_all(part, "pb", 0, 0, tiled=True)


def local(
    adjoint_source, deviation, relax_time, band_window, pair_src, pair_dst, bucket_fill, coupling
):
    states = band_window.shape[0]
    slots = pair_src.shape[0]
    pools = lax.axis_size("pool")
    window = band_window.reshape(1, states)
    src = pair_src.reshape(1, slots)
    dst = pair_dst.reshape(1, slots)
    sds = jax.ShapeDtypeStruct
    flat = pltpu.VMEM((slots, WIDTH), F32)
    partial = sds((lax.axis_size("pb"), 8, states * 3 // 2), F32)

    cost = pl.CostEstimate(flops=10**10, bytes_accessed=0, transcendentals=0)
    zero = call(zero_kernel, sds((8, 128), F32), [], cost=cost)
    sent = call(
        first_kernel, sds((pools, 128), F32), [flat],
        zero, coupling, adjoint_source, relax_time, window, src, dst, bucket_fill,
    )
    index = exchange(sent)
    gather = functools.partial(gather_kernel, states=states)
    parts = share(call(gather, partial, [], index, index))
    sent = call(
        second_kernel, sds((2 * pools, 128), F32), [flat],
        parts, index, deviation, adjoint_source, relax_time, window, src, bucket_fill, coupling,
    )
    rows = exchange(sent)
    parts = share(call(gather, partial, [], rows, index))
    return call(
        last_kernel, (sds(adjoint_source.shape, F32), sds(coupling.shape, F32)), [flat],
        parts, rows, adjoint_source, relax_time, window, src, bucket_fill,
    )


def solution(mesh):
    in_specs = (
        P(None, None, "pool"),
        P(None, None, "pool"),
        P(None, "pool"),
        P("pool"),
        P(("pool", "pb")),
        P(("pool", "pb")),
        P(("pool", "pb"), None),
        P(None, ("pool", "pb")),
    )
    out_specs = (P(None, None, "pool"), P(None, ("pool", "pb")))
    return jax.shard_map(local, mesh=mesh, in_specs=in_specs, out_specs=out_specs, check_vma=False)
```

```python
import functools

import jax
import jax.numpy as jnp
from jax import lax
from jax.experimental import pallas as pl
from jax.experimental.pallas import tpu as pltpu
from jax.sharding import PartitionSpec as P

ITERS = 2
WIDTH = 16
F32 = jnp.float32
BF16 = jnp.bfloat16
MIB = 1024 * 1024


def split3(x):
    high = x.astype(BF16)
    rest = x - high.astype(F32)
    middle = rest.astype(BF16)
    low = (rest - middle.astype(F32)).astype(BF16)
    return jnp.concatenate([high, middle, low], axis=0)


def tiles_of(x):
    parts = split3(x)
    width = min(128, x.shape[1])
    return jnp.concatenate([parts[:, t : t + width] for t in range(0, x.shape[1], width)], axis=0)


def whole(parts):
    return parts[:16] + parts[16:32] + parts[32:48]


def select(x, index):
    width = min(128, x.shape[1])
    rows = lax.broadcasted_iota(jnp.int32, (width, index.shape[1]), 0)
    hot = jnp.where(rows == (index & (width - 1)), 1.0, 0.0).astype(BF16)
    found = jnp.dot(tiles_of(x), hot, preferred_element_type=F32)
    at = jnp.broadcast_to(index, (16, index.shape[1])) >> (width.bit_length() - 1)
    total = whole(found[:48])
    for tile in range(1, x.shape[1] // width):
        total = jnp.where(at == tile, whole(found[48 * tile : 48 * tile + 48]), total)
    return total


def pick(x, index):
    parts = []
    width = min(128, index.shape[1])
    for first in range(0, index.shape[1], width):
        at = jnp.broadcast_to(index[:, first : first + width], (x.shape[0], width))
        part = jnp.zeros(at.shape, F32)
        for tile in range(x.shape[1] // 128):
            columns = x[:, 128 * tile : 128 * (tile + 1)]
            found = jnp.take_along_axis(columns, at & 127, axis=1, mode="promise_in_bounds")
            part = jnp.where(at >> 7 == tile, found, part)
        parts.append(part)
    return jnp.concatenate(parts, axis=1)


def rows16(ref):
    return jnp.concatenate([ref[0], ref[1], ref[2], jnp.zeros_like(ref[0])], axis=0)


def window16(window_ref):
    rows = lax.broadcasted_iota(jnp.int32, (16, window_ref.shape[1]), 0)
    return ((window_ref[...] >> (rows & 3)) & 1).astype(F32)


def live_row(fill_ref, slots):
    owners = fill_ref.shape[1]
    capacity = slots // owners
    fill = jnp.broadcast_to(fill_ref[...].astype(F32), (8, owners))
    lane = lax.broadcasted_iota(jnp.int32, (8, owners), 1)
    place = (lane & (capacity - 1)).astype(F32)
    parts = []
    for first in range(0, owners, owners // capacity):
        filled = jnp.take_along_axis(fill, first + (lane >> (capacity.bit_length() - 1)), axis=1, mode="promise_in_bounds")
        parts.append(jnp.where(place < filled, 1.0, 0.0)[:1])
    return jnp.concatenate(parts, axis=1)


def repeat_rows(x, first, step, count):
    row = lax.broadcasted_iota(jnp.int32, (16, x.shape[1]), 0)
    out = jnp.broadcast_to(x[first : first + 1], row.shape)
    for i in range(1, count):
        out = jnp.where(row >= 4 * i, x[first + step * i : first + step * i + 1], out)
    return out


def tile_rows(x, first):
    start = first // 8 * 8
    half = x[start : start + 8]
    turned = pltpu.roll(half, 4, 0)
    low = lax.broadcasted_iota(jnp.int32, half.shape, 0) < 4
    out = jnp.where(low, half, turned) if first == start else jnp.where(low, turned, half)
    return jnp.concatenate([out, out], axis=0)


def scatter_terms(picked, live, couple):
    total = None
    for band in range(4):
        term = tile_rows(couple, 4 * band) * repeat_rows(picked, band, 4, 3)
        total = term if total is None else total + term
    return total * live


def slots_to_rows(x, flat_ref):
    owners = x.shape[1] // 8
    flat_ref[...] = x.T
    return jnp.concatenate([flat_ref[pl.ds(j, owners, stride=8), :] for j in range(8)], axis=1)


def pack(x):
    half = x.shape[1] // 2
    tail = jnp.concatenate([x[8:12, :half], x[8:12, half:]], axis=0)
    return jnp.concatenate([x[:8], tail], axis=1)


def unpack(x):
    whole = x.shape[1] * 2 // 3
    tail = jnp.concatenate([x[:4, whole:], x[4:, whole:]], axis=1)
    return jnp.concatenate([x[:8, :whole], jnp.concatenate([tail, jnp.zeros_like(tail)], axis=0)], axis=0)


def received_slots(rows):
    turned = rows.T
    return jnp.concatenate([turned[WIDTH * j : WIDTH * (j + 1)] for j in range(8)], axis=1)


def received_hot(rows, states):
    width = min(256, states)
    lane = lax.broadcasted_iota(jnp.int32, (rows.shape[0], width), 1).astype(F32).astype(BF16)
    blocks = []
    for j in range(8):
        column = rows[:, WIDTH * j + 12 : WIDTH * j + 13]
        parts = [
            jnp.where((column - first).astype(BF16) == lane, jnp.ones_like(lane), jnp.zeros_like(lane))
            for first in range(0, states, width)
        ]
        blocks.append(jnp.concatenate(parts, axis=1))
    return jnp.concatenate(blocks, axis=0)


def zero_kernel(out_ref):
    out_ref[...] = jnp.zeros_like(out_ref)


def first_kernel(
    zero_ref, couple_ref, source_ref, relax_ref, window_ref, src_ref, dst_ref, fill_ref, out_ref, flat_ref
):
    live = live_row(fill_ref, src_ref.shape[1])
    relax = jnp.concatenate([relax_ref[...]] * 4, axis=0)
    moment = rows16(source_ref) * window16(window_ref) * relax
    terms = scatter_terms(pick(moment, src_ref[...]), live, couple_ref[...])
    row = lax.broadcasted_iota(jnp.int32, terms.shape, 0)
    terms = jnp.where(row == 12, dst_ref[...].astype(F32) + zero_ref[:1, :1], terms)
    out_ref[...] = slots_to_rows(terms, flat_ref)


def gather_kernel(rows_ref, index_ref, out_ref, *, states):
    senders = index_ref.shape[0]
    depth = rows_ref.shape[0] // senders
    rows = rows_ref[...] if depth == 1 else rows_ref[pl.ds(0, senders, stride=depth), :]
    hot = received_hot(index_ref[...], states)
    packed = pack(whole(jnp.dot(split3(received_slots(rows)), hot, preferred_element_type=F32)))
    for i in range(out_ref.shape[0]):
        out_ref[i] = packed


def returned_rows(dev_ref, window_ref, index_ref):
    masked = rows16(dev_ref) * window16(window_ref)
    turned = index_ref[...].T.astype(jnp.int32)
    found = [pick(masked, turned[WIDTH * j + 12 : WIDTH * j + 13]) for j in range(8)]
    return jnp.concatenate(found, axis=0).T


def multiplier_of(part, source_ref, window_ref):
    window = window16(window_ref)
    return window * (rows16(source_ref) + unpack((part[0] + part[1]) + (part[2] + part[3])))


def second_kernel(
    parts_ref, index_ref, dev_ref, source_ref, relax_ref, window_ref, src_ref, fill_ref, couple_ref, out_ref, flat_ref
):
    senders = index_ref.shape[0]
    out_ref[pl.ds(1, senders, stride=2), :] = returned_rows(dev_ref, window_ref, index_ref)
    relax = jnp.concatenate([relax_ref[...]] * 4, axis=0)
    moment = relax * multiplier_of(parts_ref, source_ref, window_ref)
    live = live_row(fill_ref, src_ref.shape[1])
    terms = scatter_terms(select(moment, src_ref[...]), live, couple_ref[...])
    out_ref[pl.ds(0, senders, stride=2), :] = slots_to_rows(terms, flat_ref)


def last_kernel(
    parts_ref, rows_ref, source_ref, relax_ref, window_ref, src_ref, fill_ref, multiplier_ref, grad_ref, flat_ref
):
    owners = rows_ref.shape[0] // 2
    rows = rows_ref[pl.ds(1, owners, stride=2), :]
    for j in range(8):
        flat_ref[pl.ds(j, owners, stride=8), :] = rows[:, WIDTH * j : WIDTH * (j + 1)]
    fetched = flat_ref[...].T
    relax = jnp.concatenate([relax_ref[...]] * 4, axis=0)
    multiplier = multiplier_of(parts_ref, source_ref, window_ref)
    for d in range(3):
        multiplier_ref[d] = multiplier[4 * d : 4 * d + 4]
    picked = select(relax * multiplier, src_ref[...])
    total = None
    for d in range(3):
        term = repeat_rows(picked, 4 * d, 1, 4) * tile_rows(fetched, 4 * d)
        total = term if total is None else total + term
    grad_ref[...] = total * live_row(fill_ref, src_ref.shape[1])


def call(kernel, out_shape, scratch, *operands, cost=None):
    return pl.pallas_call(
        kernel,
        out_shape=out_shape,
        in_specs=[pl.BlockSpec(memory_space=pltpu.VMEM)] * len(operands),
        scratch_shapes=scratch,
        compiler_params=pltpu.CompilerParams(vmem_limit_bytes=24 * MIB),
        cost_estimate=cost,
    )(*operands)


def exchange(rows):
    pools = lax.axis_size("pool")
    x = rows.reshape(pools, 1, -1)
    return lax.all_to_all(x, "pool", 0, 0, tiled=True).reshape(rows.shape)


def share(part):
    return lax.all_to_all(part, "pb", 0, 0, tiled=True)


def local(
    adjoint_source, deviation, relax_time, band_window, pair_src, pair_dst, bucket_fill, coupling
):
    states = band_window.shape[0]
    slots = pair_src.shape[0]
    pools = lax.axis_size("pool")
    window = band_window.reshape(1, states)
    src = pair_src.reshape(1, slots)
    dst = pair_dst.reshape(1, slots)
    sds = jax.ShapeDtypeStruct
    flat = pltpu.VMEM((slots, WIDTH), F32)
    partial = sds((lax.axis_size("pb"), 8, states * 3 // 2), F32)

    cost = pl.CostEstimate(flops=10**10, bytes_accessed=0, transcendentals=0)
    zero = call(zero_kernel, sds((8, 128), F32), [], cost=cost)
    sent = call(
        first_kernel, sds((pools, 128), F32), [flat],
        zero, coupling, adjoint_source, relax_time, window, src, dst, bucket_fill,
    )
    index = exchange(sent)
    gather = functools.partial(gather_kernel, states=states)
    parts = share(call(gather, partial, [], index, index))
    sent = call(
        second_kernel, sds((2 * pools, 128), F32), [flat],
        parts, index, deviation, adjoint_source, relax_time, window, src, bucket_fill, coupling,
    )
    rows = exchange(sent)
    parts = share(call(gather, partial, [], rows, index))
    return call(
        last_kernel, (sds(adjoint_source.shape, F32), sds(coupling.shape, F32)), [flat],
        parts, rows, adjoint_source, relax_time, window, src, bucket_fill,
    )


def solution(mesh):
    in_specs = (
        P(None, None, "pool"),
        P(None, None, "pool"),
        P(None, "pool"),
        P("pool"),
        P(("pool", "pb")),
        P(("pool", "pb")),
        P(("pool", "pb"), None),
        P(None, ("pool", "pb")),
    )
    out_specs = (P(None, None, "pool"), P(None, ("pool", "pb")))
    return jax.shard_map(local, mesh=mesh, in_specs=in_specs, out_specs=out_specs, check_vma=False)
```

```python
import functools

import jax
import jax.numpy as jnp
from jax import lax
from jax.experimental import pallas as pl
from jax.experimental.pallas import tpu as pltpu
from jax.sharding import PartitionSpec as P

ITERS = 2
WIDTH = 16
F32 = jnp.float32
BF16 = jnp.bfloat16
MIB = 1024 * 1024


def split3(x):
    high = x.astype(BF16)
    rest = x - high.astype(F32)
    middle = rest.astype(BF16)
    low = (rest - middle.astype(F32)).astype(BF16)
    return jnp.concatenate([high, middle, low], axis=0)


def tiles_of(x):
    parts = split3(x)
    width = min(128, x.shape[1])
    return jnp.concatenate([parts[:, t : t + width] for t in range(0, x.shape[1], width)], axis=0)


def whole(parts):
    return parts[:16] + parts[16:32] + parts[32:48]


def select(x, index):
    width = min(128, x.shape[1])
    rows = lax.broadcasted_iota(jnp.int32, (width, index.shape[1]), 0)
    hot = jnp.where(rows == (index & (width - 1)), 1.0, 0.0).astype(BF16)
    found = jnp.dot(tiles_of(x), hot, preferred_element_type=F32)
    at = jnp.broadcast_to(index, (16, index.shape[1])) >> (width.bit_length() - 1)
    total = whole(found[:48])
    for tile in range(1, x.shape[1] // width):
        total = jnp.where(at == tile, whole(found[48 * tile : 48 * tile + 48]), total)
    return total


def pick(x, index):
    parts = []
    width = min(128, index.shape[1])
    for first in range(0, index.shape[1], width):
        at = jnp.broadcast_to(index[:, first : first + width], (x.shape[0], width))
        part = jnp.zeros(at.shape, F32)
        for tile in range(x.shape[1] // 128):
            columns = x[:, 128 * tile : 128 * (tile + 1)]
            found = jnp.take_along_axis(columns, at & 127, axis=1, mode="promise_in_bounds")
            part = jnp.where(at >> 7 == tile, found, part)
        parts.append(part)
    return jnp.concatenate(parts, axis=1)


def rows16(ref):
    return jnp.concatenate([ref[0], ref[1], ref[2], jnp.zeros_like(ref[0])], axis=0)


def window16(window_ref):
    rows = lax.broadcasted_iota(jnp.int32, (16, window_ref.shape[1]), 0)
    return ((window_ref[...] >> (rows & 3)) & 1).astype(F32)


def live_row(fill_ref, slots):
    owners = fill_ref.shape[1]
    capacity = slots // owners
    fill = jnp.broadcast_to(fill_ref[...].astype(F32), (8, owners))
    lane = lax.broadcasted_iota(jnp.int32, (8, owners), 1)
    place = (lane & (capacity - 1)).astype(F32)
    parts = []
    for first in range(0, owners, owners // capacity):
        filled = jnp.take_along_axis(fill, first + (lane >> (capacity.bit_length() - 1)), axis=1, mode="promise_in_bounds")
        parts.append(jnp.where(place < filled, 1.0, 0.0)[:1])
    return jnp.concatenate(parts, axis=1)


def repeat_rows(x, first, step, count):
    row = lax.broadcasted_iota(jnp.int32, (16, x.shape[1]), 0)
    out = jnp.broadcast_to(x[first : first + 1], row.shape)
    for i in range(1, count):
        out = jnp.where(row >= 4 * i, x[first + step * i : first + step * i + 1], out)
    return out


def scatter_terms(picked, live, couple):
    total = None
    for band in range(4):
        block = couple[4 * band : 4 * band + 4]
        block = jnp.concatenate([block, block, block, jnp.zeros_like(block)], axis=0)
        term = block * repeat_rows(picked, band, 4, 3)
        total = term if total is None else total + term
    return total * live


def slots_to_rows(x, flat_ref):
    owners = x.shape[1] // 8
    flat_ref[...] = x.T
    return jnp.concatenate([flat_ref[pl.ds(j, owners, stride=8), :] for j in range(8)], axis=1)


def first_member(pools):
    return pools * 13 // 16


def rotate(rows, start):
    return jnp.concatenate([rows[start:], rows[:start]], axis=0)


def pack(x):
    half = x.shape[1] // 2
    tail = jnp.concatenate([x[8:12, :half], x[8:12, half:]], axis=0)
    return jnp.concatenate([x[:8], tail], axis=1)


def unpack(x):
    whole = x.shape[1] * 2 // 3
    tail = jnp.concatenate([x[:4, whole:], x[4:, whole:]], axis=1)
    return jnp.concatenate([x[:8, :whole], jnp.concatenate([tail, jnp.zeros_like(tail)], axis=0)], axis=0)


def received_slots(rows):
    turned = rows.T
    return jnp.concatenate([turned[WIDTH * j : WIDTH * (j + 1)] for j in range(8)], axis=1)


def received_hot(rows, states):
    width = min(256, states)
    lane = lax.broadcasted_iota(jnp.int32, (rows.shape[0], width), 1).astype(F32).astype(BF16)
    blocks = []
    for j in range(8):
        column = rows[:, WIDTH * j + 12 : WIDTH * j + 13]
        parts = [
            jnp.where((column - first).astype(BF16) == lane, jnp.ones_like(lane), jnp.zeros_like(lane))
            for first in range(0, states, width)
        ]
        blocks.append(jnp.concatenate(parts, axis=1))
    return jnp.concatenate(blocks, axis=0)


def zero_kernel(out_ref):
    out_ref[...] = jnp.zeros_like(out_ref)


def first_kernel(
    zero_ref, couple_ref, source_ref, relax_ref, window_ref, src_ref, dst_ref, fill_ref, out_ref, flat_ref
):
    live = live_row(fill_ref, src_ref.shape[1])
    relax = jnp.concatenate([relax_ref[...]] * 4, axis=0)
    moment = rows16(source_ref) * window16(window_ref) * relax
    terms = scatter_terms(pick(moment, src_ref[...]), live, couple_ref[...])
    row = lax.broadcasted_iota(jnp.int32, terms.shape, 0)
    terms = jnp.where(row == 12, dst_ref[...].astype(F32) + zero_ref[:1, :1], terms)
    out_ref[...] = rotate(slots_to_rows(terms, flat_ref), first_member(out_ref.shape[0]))


def gather_kernel(rows_ref, index_ref, out_ref, *, states):
    senders = index_ref.shape[0]
    depth = rows_ref.shape[0] // senders
    rows = rows_ref[...] if depth == 1 else rows_ref[pl.ds(0, senders, stride=depth), :]
    hot = received_hot(index_ref[...], states)
    packed = pack(whole(jnp.dot(split3(received_slots(rows)), hot, preferred_element_type=F32)))
    for i in range(out_ref.shape[0]):
        out_ref[i] = packed


def returned_rows(dev_ref, window_ref, index_ref):
    masked = rows16(dev_ref) * window16(window_ref)
    turned = index_ref[...].T.astype(jnp.int32)
    found = [pick(masked, turned[WIDTH * j + 12 : WIDTH * j + 13]) for j in range(8)]
    return jnp.concatenate(found, axis=0).T


def multiplier_of(part, source_ref, window_ref):
    window = window16(window_ref)
    return window * (rows16(source_ref) + unpack((part[0] + part[1]) + (part[2] + part[3])))


def second_kernel(
    parts_ref, index_ref, dev_ref, source_ref, relax_ref, window_ref, src_ref, fill_ref, couple_ref, out_ref, flat_ref
):
    senders = index_ref.shape[0]
    out_ref[pl.ds(1, senders, stride=2), :] = returned_rows(dev_ref, window_ref, index_ref)
    relax = jnp.concatenate([relax_ref[...]] * 4, axis=0)
    moment = relax * multiplier_of(parts_ref, source_ref, window_ref)
    live = live_row(fill_ref, src_ref.shape[1])
    terms = scatter_terms(select(moment, src_ref[...]), live, couple_ref[...])
    rows = rotate(slots_to_rows(terms, flat_ref), first_member(senders))
    out_ref[pl.ds(0, senders, stride=2), :] = rows


def last_kernel(
    parts_ref, rows_ref, source_ref, relax_ref, window_ref, src_ref, fill_ref, multiplier_ref, grad_ref, flat_ref
):
    owners = rows_ref.shape[0] // 2
    rows = rotate(rows_ref[pl.ds(1, owners, stride=2), :], owners - first_member(owners))
    for j in range(8):
        flat_ref[pl.ds(j, owners, stride=8), :] = rows[:, WIDTH * j : WIDTH * (j + 1)]
    fetched = flat_ref[...].T
    relax = jnp.concatenate([relax_ref[...]] * 4, axis=0)
    multiplier = multiplier_of(parts_ref, source_ref, window_ref)
    for d in range(3):
        multiplier_ref[d] = multiplier[4 * d : 4 * d + 4]
    picked = select(relax * multiplier, src_ref[...])
    total = None
    for d in range(3):
        far = fetched[4 * d : 4 * d + 4]
        term = repeat_rows(picked, 4 * d, 1, 4) * jnp.concatenate([far] * 4, axis=0)
        total = term if total is None else total + term
    grad_ref[...] = total * live_row(fill_ref, src_ref.shape[1])


def call(kernel, out_shape, scratch, *operands, cost=None):
    return pl.pallas_call(
        kernel,
        out_shape=out_shape,
        in_specs=[pl.BlockSpec(memory_space=pltpu.VMEM)] * len(operands),
        scratch_shapes=scratch,
        compiler_params=pltpu.CompilerParams(vmem_limit_bytes=24 * MIB),
        cost_estimate=cost,
    )(*operands)


def exchange(rows):
    pools = lax.axis_size("pool")
    members = [[(place + first_member(pools)) % pools for place in range(pools)]]
    x = rows.reshape(pools, -1, 128)
    x = lax.all_to_all(x, "pool", 0, 0, axis_index_groups=members, tiled=True)
    return x.reshape(rows.shape)


def share(part):
    return lax.all_to_all(part, "pb", 0, 0, tiled=True)


def local(
    adjoint_source, deviation, relax_time, band_window, pair_src, pair_dst, bucket_fill, coupling
):
    states = band_window.shape[0]
    slots = pair_src.shape[0]
    pools = lax.axis_size("pool")
    window = band_window.reshape(1, states)
    src = pair_src.reshape(1, slots)
    dst = pair_dst.reshape(1, slots)
    sds = jax.ShapeDtypeStruct
    flat = pltpu.VMEM((slots, WIDTH), F32)
    partial = sds((lax.axis_size("pb"), 8, states * 3 // 2), F32)

    cost = pl.CostEstimate(flops=10**10, bytes_accessed=0, transcendentals=0)
    zero = call(zero_kernel, sds((8, 128), F32), [], cost=cost)
    sent = call(
        first_kernel, sds((pools, 128), F32), [flat],
        zero, coupling, adjoint_source, relax_time, window, src, dst, bucket_fill,
    )
    index = exchange(sent)
    gather = functools.partial(gather_kernel, states=states)
    parts = share(call(gather, partial, [], index, index))
    sent = call(
        second_kernel, sds((2 * pools, 128), F32), [flat],
        parts, index, deviation, adjoint_source, relax_time, window, src, bucket_fill, coupling,
    )
    rows = exchange(sent)
    parts = share(call(gather, partial, [], rows, index))
    return call(
        last_kernel, (sds(adjoint_source.shape, F32), sds(coupling.shape, F32)), [flat],
        parts, rows, adjoint_source, relax_time, window, src, bucket_fill,
    )


def solution(mesh):
    in_specs = (
        P(None, None, "pool"),
        P(None, None, "pool"),
        P(None, "pool"),
        P("pool"),
        P(("pool", "pb")),
        P(("pool", "pb")),
        P(("pool", "pb"), None),
        P(None, ("pool", "pb")),
    )
    out_specs = (P(None, None, "pool"), P(None, ("pool", "pb")))
    return jax.shard_map(local, mesh=mesh, in_specs=in_specs, out_specs=out_specs, check_vma=False)
```

```python
import functools

import jax
import jax.numpy as jnp
from jax import lax
from jax.experimental import pallas as pl
from jax.experimental.pallas import tpu as pltpu
from jax.sharding import PartitionSpec as P

ITERS = 2
WIDTH = 16
F32 = jnp.float32
BF16 = jnp.bfloat16
MIB = 1024 * 1024


def split3(x):
    high = x.astype(BF16)
    rest = x - high.astype(F32)
    middle = rest.astype(BF16)
    low = (rest - middle.astype(F32)).astype(BF16)
    return jnp.concatenate([high, middle, low], axis=0)


def tiles_of(x):
    parts = split3(x)
    width = min(128, x.shape[1])
    return jnp.concatenate([parts[:, t : t + width] for t in range(0, x.shape[1], width)], axis=0)


def whole(parts):
    return parts[:16] + parts[16:32] + parts[32:48]


def select(x, index):
    width = min(128, x.shape[1])
    rows = lax.broadcasted_iota(jnp.int32, (width, index.shape[1]), 0)
    hot = jnp.where(rows == (index & (width - 1)), 1.0, 0.0).astype(BF16)
    found = jnp.dot(tiles_of(x), hot, preferred_element_type=F32)
    at = jnp.broadcast_to(index, (16, index.shape[1])) >> (width.bit_length() - 1)
    total = whole(found[:48])
    for tile in range(1, x.shape[1] // width):
        total = jnp.where(at == tile, whole(found[48 * tile : 48 * tile + 48]), total)
    return total


def pick(x, index):
    parts = []
    width = min(128, index.shape[1])
    for first in range(0, index.shape[1], width):
        at = jnp.broadcast_to(index[:, first : first + width], (x.shape[0], width))
        part = jnp.zeros(at.shape, F32)
        for tile in range(x.shape[1] // 128):
            columns = x[:, 128 * tile : 128 * (tile + 1)]
            found = jnp.take_along_axis(columns, at & 127, axis=1, mode="promise_in_bounds")
            part = jnp.where(at >> 7 == tile, found, part)
        parts.append(part)
    return jnp.concatenate(parts, axis=1)


def rows16(ref):
    return jnp.concatenate([ref[0], ref[1], ref[2], jnp.zeros_like(ref[0])], axis=0)


def window16(window_ref):
    rows = lax.broadcasted_iota(jnp.int32, (16, window_ref.shape[1]), 0)
    return ((window_ref[...] >> (rows & 3)) & 1).astype(F32)


def live_row(fill_ref, slots):
    owners = fill_ref.shape[1]
    capacity = slots // owners
    fill = jnp.broadcast_to(fill_ref[...].astype(F32), (8, owners))
    lane = lax.broadcasted_iota(jnp.int32, (8, owners), 1)
    place = (lane & (capacity - 1)).astype(F32)
    parts = []
    for first in range(0, owners, owners // capacity):
        filled = jnp.take_along_axis(fill, first + (lane >> (capacity.bit_length() - 1)), axis=1, mode="promise_in_bounds")
        parts.append(jnp.where(place < filled, 1.0, 0.0)[:1])
    return jnp.concatenate(parts, axis=1)


def repeat_rows(x, first, step, count):
    row = lax.broadcasted_iota(jnp.int32, (16, x.shape[1]), 0)
    out = jnp.broadcast_to(x[first : first + 1], row.shape)
    for i in range(1, count):
        out = jnp.where(row >= 4 * i, x[first + step * i : first + step * i + 1], out)
    return out


def scatter_terms(picked, live, couple):
    total = None
    for band in range(4):
        block = couple[4 * band : 4 * band + 4]
        block = jnp.concatenate([block, block, block, jnp.zeros_like(block)], axis=0)
        term = block * repeat_rows(picked, band, 4, 3)
        total = term if total is None else total + term
    return total * live


def slots_to_rows(x, flat_ref):
    owners = x.shape[1] // 8
    flat_ref[...] = x.T
    return jnp.concatenate([flat_ref[pl.ds(j, owners, stride=8), :] for j in range(8)], axis=1)


def first_chip(pools):
    return pools * 13 // 16


def to_places(rows):
    start = first_chip(rows.shape[0])
    return jnp.concatenate([rows[start + 1 : start + 2], rows[start : start + 1], rows[start + 2 :], rows[:start]], axis=0)


def from_places(rows):
    rest = rows.shape[0] - first_chip(rows.shape[0])
    return jnp.concatenate([rows[rest:], rows[1:2], rows[:1], rows[2:rest]], axis=0)


def pack(x):
    half = x.shape[1] // 2
    tail = jnp.concatenate([x[8:12, :half], x[8:12, half:]], axis=0)
    return jnp.concatenate([x[:8], tail], axis=1)


def unpack(x):
    whole = x.shape[1] * 2 // 3
    tail = jnp.concatenate([x[:4, whole:], x[4:, whole:]], axis=1)
    return jnp.concatenate([x[:8, :whole], jnp.concatenate([tail, jnp.zeros_like(tail)], axis=0)], axis=0)


def received_slots(rows):
    turned = rows.T
    return jnp.concatenate([turned[WIDTH * j : WIDTH * (j + 1)] for j in range(8)], axis=1)


def received_hot(rows, states):
    width = min(256, states)
    lane = lax.broadcasted_iota(jnp.int32, (rows.shape[0], width), 1).astype(F32).astype(BF16)
    blocks = []
    for j in range(8):
        column = rows[:, WIDTH * j + 12 : WIDTH * j + 13]
        parts = [
            jnp.where((column - first).astype(BF16) == lane, jnp.ones_like(lane), jnp.zeros_like(lane))
            for first in range(0, states, width)
        ]
        blocks.append(jnp.concatenate(parts, axis=1))
    return jnp.concatenate(blocks, axis=0)


def zero_kernel(out_ref):
    out_ref[...] = jnp.zeros_like(out_ref)


def first_kernel(
    zero_ref, couple_ref, source_ref, relax_ref, window_ref, src_ref, dst_ref, fill_ref, out_ref, flat_ref
):
    live = live_row(fill_ref, src_ref.shape[1])
    relax = jnp.concatenate([relax_ref[...]] * 4, axis=0)
    moment = rows16(source_ref) * window16(window_ref) * relax
    terms = scatter_terms(pick(moment, src_ref[...]), live, couple_ref[...])
    row = lax.broadcasted_iota(jnp.int32, terms.shape, 0)
    terms = jnp.where(row == 12, dst_ref[...].astype(F32) + zero_ref[:1, :1], terms)
    out_ref[...] = to_places(slots_to_rows(terms, flat_ref))


def gather_kernel(rows_ref, index_ref, out_ref, *, states):
    senders = index_ref.shape[0]
    depth = rows_ref.shape[0] // senders
    rows = rows_ref[...] if depth == 1 else rows_ref[pl.ds(0, senders, stride=depth), :]
    hot = received_hot(index_ref[...], states)
    packed = pack(whole(jnp.dot(split3(received_slots(rows)), hot, preferred_element_type=F32)))
    for i in range(out_ref.shape[0]):
        out_ref[i] = packed


def returned_rows(dev_ref, window_ref, index_ref):
    masked = rows16(dev_ref) * window16(window_ref)
    turned = index_ref[...].T.astype(jnp.int32)
    found = [pick(masked, turned[WIDTH * j + 12 : WIDTH * j + 13]) for j in range(8)]
    return jnp.concatenate(found, axis=0).T


def multiplier_of(part, source_ref, window_ref):
    window = window16(window_ref)
    return window * (rows16(source_ref) + unpack((part[0] + part[1]) + (part[2] + part[3])))


def second_kernel(
    parts_ref, index_ref, dev_ref, source_ref, relax_ref, window_ref, src_ref, fill_ref, couple_ref, out_ref, flat_ref
):
    senders = index_ref.shape[0]
    out_ref[pl.ds(1, senders, stride=2), :] = returned_rows(dev_ref, window_ref, index_ref)
    relax = jnp.concatenate([relax_ref[...]] * 4, axis=0)
    moment = relax * multiplier_of(parts_ref, source_ref, window_ref)
    live = live_row(fill_ref, src_ref.shape[1])
    terms = scatter_terms(select(moment, src_ref[...]), live, couple_ref[...])
    rows = to_places(slots_to_rows(terms, flat_ref))
    out_ref[pl.ds(0, senders, stride=2), :] = rows


def last_kernel(
    parts_ref, rows_ref, source_ref, relax_ref, window_ref, src_ref, fill_ref, multiplier_ref, grad_ref, flat_ref
):
    owners = rows_ref.shape[0] // 2
    rows = from_places(rows_ref[pl.ds(1, owners, stride=2), :])
    for j in range(8):
        flat_ref[pl.ds(j, owners, stride=8), :] = rows[:, WIDTH * j : WIDTH * (j + 1)]
    fetched = flat_ref[...].T
    relax = jnp.concatenate([relax_ref[...]] * 4, axis=0)
    multiplier = multiplier_of(parts_ref, source_ref, window_ref)
    for d in range(3):
        multiplier_ref[d] = multiplier[4 * d : 4 * d + 4]
    picked = select(relax * multiplier, src_ref[...])
    total = None
    for d in range(3):
        far = fetched[4 * d : 4 * d + 4]
        term = repeat_rows(picked, 4 * d, 1, 4) * jnp.concatenate([far] * 4, axis=0)
        total = term if total is None else total + term
    grad_ref[...] = total * live_row(fill_ref, src_ref.shape[1])


def call(kernel, out_shape, scratch, *operands, cost=None):
    return pl.pallas_call(
        kernel,
        out_shape=out_shape,
        in_specs=[pl.BlockSpec(memory_space=pltpu.VMEM)] * len(operands),
        scratch_shapes=scratch,
        compiler_params=pltpu.CompilerParams(vmem_limit_bytes=24 * MIB),
        cost_estimate=cost,
    )(*operands)


def exchange(rows):
    pools = lax.axis_size("pool")
    members = [(place + first_chip(pools)) % pools for place in range(pools)]
    members[:2] = members[1::-1]
    x = rows.reshape(pools, -1, 128)
    x = lax.all_to_all(x, "pool", 0, 0, axis_index_groups=[members], tiled=True)
    return x.reshape(rows.shape)


def share(part):
    groups = lax.axis_size("pb")
    members = [(place + groups // 2) % groups for place in range(groups)]
    return lax.all_to_all(part, "pb", 0, 0, axis_index_groups=[members], tiled=True)


def local(
    adjoint_source, deviation, relax_time, band_window, pair_src, pair_dst, bucket_fill, coupling
):
    states = band_window.shape[0]
    slots = pair_src.shape[0]
    pools = lax.axis_size("pool")
    window = band_window.reshape(1, states)
    src = pair_src.reshape(1, slots)
    dst = pair_dst.reshape(1, slots)
    sds = jax.ShapeDtypeStruct
    flat = pltpu.VMEM((slots, WIDTH), F32)
    partial = sds((lax.axis_size("pb"), 8, states * 3 // 2), F32)

    cost = pl.CostEstimate(flops=10**10, bytes_accessed=0, transcendentals=0)
    zero = call(zero_kernel, sds((8, 128), F32), [], cost=cost)
    sent = call(
        first_kernel, sds((pools, 128), F32), [flat],
        zero, coupling, adjoint_source, relax_time, window, src, dst, bucket_fill,
    )
    index = exchange(sent)
    gather = functools.partial(gather_kernel, states=states)
    parts = share(call(gather, partial, [], index, index))
    sent = call(
        second_kernel, sds((2 * pools, 128), F32), [flat],
        parts, index, deviation, adjoint_source, relax_time, window, src, bucket_fill, coupling,
    )
    rows = exchange(sent)
    parts = share(call(gather, partial, [], rows, index))
    return call(
        last_kernel, (sds(adjoint_source.shape, F32), sds(coupling.shape, F32)), [flat],
        parts, rows, adjoint_source, relax_time, window, src, bucket_fill,
    )


def solution(mesh):
    in_specs = (
        P(None, None, "pool"),
        P(None, None, "pool"),
        P(None, "pool"),
        P("pool"),
        P(("pool", "pb")),
        P(("pool", "pb")),
        P(("pool", "pb"), None),
        P(None, ("pool", "pb")),
    )
    out_specs = (P(None, None, "pool"), P(None, ("pool", "pb")))
    return jax.shard_map(local, mesh=mesh, in_specs=in_specs, out_specs=out_specs, check_vma=False)
```

```python
import functools

import jax
import jax.numpy as jnp
from jax import lax
from jax.experimental import pallas as pl
from jax.experimental.pallas import tpu as pltpu
from jax.sharding import PartitionSpec as P

ITERS = 2
WIDTH = 16
F32 = jnp.float32
BF16 = jnp.bfloat16
MIB = 1024 * 1024


def split3(x):
    high = x.astype(BF16)
    rest = x - high.astype(F32)
    middle = rest.astype(BF16)
    low = (rest - middle.astype(F32)).astype(BF16)
    return jnp.concatenate([high, middle, low], axis=0)


def tiles_of(x):
    parts = split3(x)
    width = min(128, x.shape[1])
    return jnp.concatenate([parts[:, t : t + width] for t in range(0, x.shape[1], width)], axis=0)


def whole(parts):
    return parts[:16] + parts[16:32] + parts[32:48]


def select(x, index):
    width = min(128, x.shape[1])
    rows = lax.broadcasted_iota(jnp.int32, (width, index.shape[1]), 0)
    hot = jnp.where(rows == (index & (width - 1)), 1.0, 0.0).astype(BF16)
    found = jnp.dot(tiles_of(x), hot, preferred_element_type=F32)
    at = jnp.broadcast_to(index, (16, index.shape[1])) >> (width.bit_length() - 1)
    total = whole(found[:48])
    for tile in range(1, x.shape[1] // width):
        total = jnp.where(at == tile, whole(found[48 * tile : 48 * tile + 48]), total)
    return total


def pick(x, index):
    parts = []
    width = min(128, index.shape[1])
    for first in range(0, index.shape[1], width):
        at = jnp.broadcast_to(index[:, first : first + width], (x.shape[0], width))
        part = jnp.zeros(at.shape, F32)
        for tile in range(x.shape[1] // 128):
            columns = x[:, 128 * tile : 128 * (tile + 1)]
            found = jnp.take_along_axis(columns, at & 127, axis=1, mode="promise_in_bounds")
            part = jnp.where(at >> 7 == tile, found, part)
        parts.append(part)
    return jnp.concatenate(parts, axis=1)


def rows16(ref):
    return jnp.concatenate([ref[0], ref[1], ref[2], jnp.zeros_like(ref[0])], axis=0)


def window16(window_ref):
    rows = lax.broadcasted_iota(jnp.int32, (16, window_ref.shape[1]), 0)
    return ((window_ref[...] >> (rows & 3)) & 1).astype(F32)


def live_row(fill_ref, slots):
    owners = fill_ref.shape[1]
    capacity = slots // owners
    fill = jnp.broadcast_to(fill_ref[...].astype(F32), (8, owners))
    lane = lax.broadcasted_iota(jnp.int32, (8, owners), 1)
    place = (lane & (capacity - 1)).astype(F32)
    parts = []
    for first in range(0, owners, owners // capacity):
        filled = jnp.take_along_axis(fill, first + (lane >> (capacity.bit_length() - 1)), axis=1, mode="promise_in_bounds")
        parts.append(jnp.where(place < filled, 1.0, 0.0)[:1])
    return jnp.concatenate(parts, axis=1)


def repeat_rows(x, first, step, count):
    row = lax.broadcasted_iota(jnp.int32, (16, x.shape[1]), 0)
    out = jnp.broadcast_to(x[first : first + 1], row.shape)
    for i in range(1, count):
        out = jnp.where(row >= 4 * i, x[first + step * i : first + step * i + 1], out)
    return out


def scatter_terms(picked, live, couple):
    total = None
    for band in range(4):
        block = couple[4 * band : 4 * band + 4]
        block = jnp.concatenate([block, block, block, jnp.zeros_like(block)], axis=0)
        term = block * repeat_rows(picked, band, 4, 3)
        total = term if total is None else total + term
    return total * live


def slots_to_rows(x, flat_ref):
    owners = x.shape[1] // 8
    flat_ref[...] = x.T
    return jnp.concatenate([flat_ref[pl.ds(j, owners, stride=8), :] for j in range(8)], axis=1)


FIRST, SECOND = 13, 9


def to_places(rows, at):
    start = rows.shape[0] * at // 16
    return jnp.concatenate([rows[start + 1 : start + 2], rows[start : start + 1], rows[start + 2 :], rows[:start]], axis=0)


def from_places(rows, at):
    rest = rows.shape[0] - rows.shape[0] * at // 16
    return jnp.concatenate([rows[rest:], rows[1:2], rows[:1], rows[2:rest]], axis=0)


def pack(x):
    half = x.shape[1] // 2
    tail = jnp.concatenate([x[8:12, :half], x[8:12, half:]], axis=0)
    return jnp.concatenate([x[:8], tail], axis=1)


def unpack(x):
    whole = x.shape[1] * 2 // 3
    tail = jnp.concatenate([x[:4, whole:], x[4:, whole:]], axis=1)
    return jnp.concatenate([x[:8, :whole], jnp.concatenate([tail, jnp.zeros_like(tail)], axis=0)], axis=0)


def received_slots(rows):
    turned = rows.T
    return jnp.concatenate([turned[WIDTH * j : WIDTH * (j + 1)] for j in range(8)], axis=1)


def received_hot(rows, states):
    width = min(256, states)
    lane = lax.broadcasted_iota(jnp.int32, (rows.shape[0], width), 1).astype(F32).astype(BF16)
    blocks = []
    for j in range(8):
        column = rows[:, WIDTH * j + 12 : WIDTH * j + 13]
        parts = [
            jnp.where((column - first).astype(BF16) == lane, jnp.ones_like(lane), jnp.zeros_like(lane))
            for first in range(0, states, width)
        ]
        blocks.append(jnp.concatenate(parts, axis=1))
    return jnp.concatenate(blocks, axis=0)


def zero_kernel(out_ref):
    out_ref[...] = jnp.zeros_like(out_ref)


def first_kernel(
    zero_ref, couple_ref, source_ref, relax_ref, window_ref, src_ref, dst_ref, fill_ref, out_ref, flat_ref
):
    live = live_row(fill_ref, src_ref.shape[1])
    relax = jnp.concatenate([relax_ref[...]] * 4, axis=0)
    moment = rows16(source_ref) * window16(window_ref) * relax
    terms = scatter_terms(pick(moment, src_ref[...]), live, couple_ref[...])
    row = lax.broadcasted_iota(jnp.int32, terms.shape, 0)
    terms = jnp.where(row == 12, dst_ref[...].astype(F32) + zero_ref[:1, :1], terms)
    out_ref[...] = to_places(slots_to_rows(terms, flat_ref), FIRST)


def gather_kernel(rows_ref, index_ref, out_ref, *, states):
    senders = index_ref.shape[0]
    depth = rows_ref.shape[0] // senders
    rows, index = rows_ref[...], index_ref[...]
    if depth > 1:
        rows = rows_ref[pl.ds(0, senders, stride=depth), :]
        index = to_places(from_places(index, FIRST), SECOND)
    hot = received_hot(index, states)
    packed = pack(whole(jnp.dot(split3(received_slots(rows)), hot, preferred_element_type=F32)))
    for i in range(out_ref.shape[0]):
        out_ref[i] = packed


def returned_rows(dev_ref, window_ref, index_ref):
    masked = rows16(dev_ref) * window16(window_ref)
    turned = index_ref[...].T.astype(jnp.int32)
    found = [pick(masked, turned[WIDTH * j + 12 : WIDTH * j + 13]) for j in range(8)]
    return jnp.concatenate(found, axis=0).T


def multiplier_of(part, source_ref, window_ref):
    window = window16(window_ref)
    return window * (rows16(source_ref) + unpack((part[0] + part[1]) + (part[2] + part[3])))


def second_kernel(
    parts_ref, index_ref, dev_ref, source_ref, relax_ref, window_ref, src_ref, fill_ref, couple_ref, out_ref, flat_ref
):
    senders = index_ref.shape[0]
    back = returned_rows(dev_ref, window_ref, index_ref)
    out_ref[pl.ds(1, senders, stride=2), :] = to_places(from_places(back, FIRST), SECOND)
    relax = jnp.concatenate([relax_ref[...]] * 4, axis=0)
    moment = relax * multiplier_of(parts_ref, source_ref, window_ref)
    live = live_row(fill_ref, src_ref.shape[1])
    terms = scatter_terms(select(moment, src_ref[...]), live, couple_ref[...])
    rows = to_places(slots_to_rows(terms, flat_ref), SECOND)
    out_ref[pl.ds(0, senders, stride=2), :] = rows


def last_kernel(
    parts_ref, rows_ref, source_ref, relax_ref, window_ref, src_ref, fill_ref, multiplier_ref, grad_ref, flat_ref
):
    owners = rows_ref.shape[0] // 2
    rows = from_places(rows_ref[pl.ds(1, owners, stride=2), :], SECOND)
    for j in range(8):
        flat_ref[pl.ds(j, owners, stride=8), :] = rows[:, WIDTH * j : WIDTH * (j + 1)]
    fetched = flat_ref[...].T
    relax = jnp.concatenate([relax_ref[...]] * 4, axis=0)
    multiplier = multiplier_of(parts_ref, source_ref, window_ref)
    for d in range(3):
        multiplier_ref[d] = multiplier[4 * d : 4 * d + 4]
    picked = select(relax * multiplier, src_ref[...])
    total = None
    for d in range(3):
        far = fetched[4 * d : 4 * d + 4]
        term = repeat_rows(picked, 4 * d, 1, 4) * jnp.concatenate([far] * 4, axis=0)
        total = term if total is None else total + term
    grad_ref[...] = total * live_row(fill_ref, src_ref.shape[1])


def call(kernel, out_shape, scratch, *operands, cost=None):
    return pl.pallas_call(
        kernel,
        out_shape=out_shape,
        in_specs=[pl.BlockSpec(memory_space=pltpu.VMEM)] * len(operands),
        scratch_shapes=scratch,
        compiler_params=pltpu.CompilerParams(vmem_limit_bytes=24 * MIB),
        cost_estimate=cost,
    )(*operands)


def exchange(rows, at):
    pools = lax.axis_size("pool")
    members = [(place + pools * at // 16) % pools for place in range(pools)]
    members[:2] = members[1::-1]
    x = rows.reshape(pools, -1, 128)
    x = lax.all_to_all(x, "pool", 0, 0, axis_index_groups=[members], tiled=True)
    return x.reshape(rows.shape)


def share(part):
    groups = lax.axis_size("pb")
    members = [(place + groups // 2) % groups for place in range(groups)]
    return lax.all_to_all(part, "pb", 0, 0, axis_index_groups=[members], tiled=True)


def local(
    adjoint_source, deviation, relax_time, band_window, pair_src, pair_dst, bucket_fill, coupling
):
    states = band_window.shape[0]
    slots = pair_src.shape[0]
    pools = lax.axis_size("pool")
    window = band_window.reshape(1, states)
    src = pair_src.reshape(1, slots)
    dst = pair_dst.reshape(1, slots)
    sds = jax.ShapeDtypeStruct
    flat = pltpu.VMEM((slots, WIDTH), F32)
    partial = sds((lax.axis_size("pb"), 8, states * 3 // 2), F32)

    cost = pl.CostEstimate(flops=10**10, bytes_accessed=0, transcendentals=0)
    zero = call(zero_kernel, sds((8, 128), F32), [], cost=cost)
    sent = call(
        first_kernel, sds((pools, 128), F32), [flat],
        zero, coupling, adjoint_source, relax_time, window, src, dst, bucket_fill,
    )
    index = exchange(sent, FIRST)
    gather = functools.partial(gather_kernel, states=states)
    parts = share(call(gather, partial, [], index, index))
    sent = call(
        second_kernel, sds((2 * pools, 128), F32), [flat],
        parts, index, deviation, adjoint_source, relax_time, window, src, bucket_fill, coupling,
    )
    rows = exchange(sent, SECOND)
    parts = share(call(gather, partial, [], rows, index))
    return call(
        last_kernel, (sds(adjoint_source.shape, F32), sds(coupling.shape, F32)), [flat],
        parts, rows, adjoint_source, relax_time, window, src, bucket_fill,
    )


def solution(mesh):
    in_specs = (
        P(None, None, "pool"),
        P(None, None, "pool"),
        P(None, "pool"),
        P("pool"),
        P(("pool", "pb")),
        P(("pool", "pb")),
        P(("pool", "pb"), None),
        P(None, ("pool", "pb")),
    )
    out_specs = (P(None, None, "pool"), P(None, ("pool", "pb")))
    return jax.shard_map(local, mesh=mesh, in_specs=in_specs, out_specs=out_specs, check_vma=False)
```

```python
import functools

import jax
import jax.numpy as jnp
from jax import lax
from jax.experimental import pallas as pl
from jax.experimental.pallas import tpu as pltpu
from jax.sharding import PartitionSpec as P

ITERS = 2
WIDTH = 16
F32 = jnp.float32
BF16 = jnp.bfloat16
MIB = 1024 * 1024


def split3(x):
    high = x.astype(BF16)
    rest = x - high.astype(F32)
    middle = rest.astype(BF16)
    low = (rest - middle.astype(F32)).astype(BF16)
    return jnp.concatenate([high, middle, low], axis=0)


def tiles_of(x):
    parts = split3(x)
    width = min(128, x.shape[1])
    return jnp.concatenate([parts[:, t : t + width] for t in range(0, x.shape[1], width)], axis=0)


def whole(parts):
    return parts[:16] + parts[16:32] + parts[32:48]


def select(x, index):
    width = min(128, x.shape[1])
    rows = lax.broadcasted_iota(jnp.int32, (width, index.shape[1]), 0)
    hot = jnp.where(rows == (index & (width - 1)), 1.0, 0.0).astype(BF16)
    found = jnp.dot(tiles_of(x), hot, preferred_element_type=F32)
    at = jnp.broadcast_to(index, (16, index.shape[1])) >> (width.bit_length() - 1)
    total = whole(found[:48])
    for tile in range(1, x.shape[1] // width):
        total = jnp.where(at == tile, whole(found[48 * tile : 48 * tile + 48]), total)
    return total


def pick(x, index):
    parts = []
    width = min(128, index.shape[1])
    for first in range(0, index.shape[1], width):
        at = jnp.broadcast_to(index[:, first : first + width], (x.shape[0], width))
        part = jnp.zeros(at.shape, F32)
        for tile in range(x.shape[1] // 128):
            columns = x[:, 128 * tile : 128 * (tile + 1)]
            found = jnp.take_along_axis(columns, at & 127, axis=1, mode="promise_in_bounds")
            part = jnp.where(at >> 7 == tile, found, part)
        parts.append(part)
    return jnp.concatenate(parts, axis=1)


def rows16(ref):
    return jnp.concatenate([ref[0], ref[1], ref[2], jnp.zeros_like(ref[0])], axis=0)


def window16(window_ref):
    rows = lax.broadcasted_iota(jnp.int32, (16, window_ref.shape[1]), 0)
    return ((window_ref[...] >> (rows & 3)) & 1).astype(F32)


def live_row(fill_ref, slots):
    owners = fill_ref.shape[1]
    capacity = slots // owners
    fill = jnp.broadcast_to(fill_ref[...].astype(F32), (8, owners))
    lane = lax.broadcasted_iota(jnp.int32, (8, owners), 1)
    place = (lane & (capacity - 1)).astype(F32)
    parts = []
    for first in range(0, owners, owners // capacity):
        filled = jnp.take_along_axis(fill, first + (lane >> (capacity.bit_length() - 1)), axis=1, mode="promise_in_bounds")
        parts.append(jnp.where(place < filled, 1.0, 0.0)[:1])
    return jnp.concatenate(parts, axis=1)


def repeat_rows(x, first, step, count):
    row = lax.broadcasted_iota(jnp.int32, (16, x.shape[1]), 0)
    out = jnp.broadcast_to(x[first : first + 1], row.shape)
    for i in range(1, count):
        out = jnp.where(row >= 4 * i, x[first + step * i : first + step * i + 1], out)
    return out


def scatter_terms(picked, live, couple):
    total = None
    for band in range(4):
        block = couple[4 * band : 4 * band + 4]
        block = jnp.concatenate([block, block, block, jnp.zeros_like(block)], axis=0)
        term = block * repeat_rows(picked, band, 4, 3)
        total = term if total is None else total + term
    return total * live


def slots_to_rows(x, flat_ref):
    owners = x.shape[1] // 8
    flat_ref[...] = x.T
    return jnp.concatenate([flat_ref[pl.ds(j, owners, stride=8), :] for j in range(8)], axis=1)


def first_chip(pools):
    return pools * 15 // 16


def to_places(rows):
    start = first_chip(rows.shape[0])
    return jnp.concatenate([rows[start + 1 : start + 2], rows[start : start + 1], rows[start + 2 :], rows[:start]], axis=0)


def from_places(rows):
    rest = rows.shape[0] - first_chip(rows.shape[0])
    return jnp.concatenate([rows[rest:], rows[1:2], rows[:1], rows[2:rest]], axis=0)


def pack(x):
    half = x.shape[1] // 2
    tail = jnp.concatenate([x[8:12, :half], x[8:12, half:]], axis=0)
    return jnp.concatenate([x[:8], tail], axis=1)


def unpack(x):
    whole = x.shape[1] * 2 // 3
    tail = jnp.concatenate([x[:4, whole:], x[4:, whole:]], axis=1)
    return jnp.concatenate([x[:8, :whole], jnp.concatenate([tail, jnp.zeros_like(tail)], axis=0)], axis=0)


def received_slots(rows):
    turned = rows.T
    return jnp.concatenate([turned[WIDTH * j : WIDTH * (j + 1)] for j in range(8)], axis=1)


def received_hot(rows, states):
    width = min(256, states)
    lane = lax.broadcasted_iota(jnp.int32, (rows.shape[0], width), 1).astype(F32).astype(BF16)
    blocks = []
    for j in range(8):
        column = rows[:, WIDTH * j + 12 : WIDTH * j + 13]
        parts = [
            jnp.where((column - first).astype(BF16) == lane, jnp.ones_like(lane), jnp.zeros_like(lane))
            for first in range(0, states, width)
        ]
        blocks.append(jnp.concatenate(parts, axis=1))
    return jnp.concatenate(blocks, axis=0)


def zero_kernel(out_ref):
    out_ref[...] = jnp.zeros_like(out_ref)


def first_kernel(
    zero_ref, couple_ref, source_ref, relax_ref, window_ref, src_ref, dst_ref, fill_ref, out_ref, flat_ref
):
    live = live_row(fill_ref, src_ref.shape[1])
    relax = jnp.concatenate([relax_ref[...]] * 4, axis=0)
    moment = rows16(source_ref) * window16(window_ref) * relax
    terms = scatter_terms(pick(moment, src_ref[...]), live, couple_ref[...])
    row = lax.broadcasted_iota(jnp.int32, terms.shape, 0)
    terms = jnp.where(row == 12, dst_ref[...].astype(F32) + zero_ref[:1, :1], terms)
    out_ref[...] = to_places(slots_to_rows(terms, flat_ref))


def gather_kernel(rows_ref, index_ref, out_ref, *, states):
    senders = index_ref.shape[0]
    depth = rows_ref.shape[0] // senders
    rows = rows_ref[...] if depth == 1 else rows_ref[pl.ds(0, senders, stride=depth), :]
    hot = received_hot(index_ref[...], states)
    packed = pack(whole(jnp.dot(split3(received_slots(rows)), hot, preferred_element_type=F32)))
    for i in range(out_ref.shape[0]):
        out_ref[i] = packed


def returned_rows(dev_ref, window_ref, index_ref):
    masked = rows16(dev_ref) * window16(window_ref)
    turned = index_ref[...].T.astype(jnp.int32)
    found = [pick(masked, turned[WIDTH * j + 12 : WIDTH * j + 13]) for j in range(8)]
    return jnp.concatenate(found, axis=0).T


def multiplier_of(part, source_ref, window_ref):
    window = window16(window_ref)
    return window * (rows16(source_ref) + unpack((part[0] + part[1]) + (part[2] + part[3])))


def second_kernel(
    parts_ref, index_ref, dev_ref, source_ref, relax_ref, window_ref, src_ref, fill_ref, couple_ref, out_ref, flat_ref
):
    senders = index_ref.shape[0]
    out_ref[pl.ds(1, senders, stride=2), :] = returned_rows(dev_ref, window_ref, index_ref)
    relax = jnp.concatenate([relax_ref[...]] * 4, axis=0)
    moment = relax * multiplier_of(parts_ref, source_ref, window_ref)
    live = live_row(fill_ref, src_ref.shape[1])
    terms = scatter_terms(select(moment, src_ref[...]), live, couple_ref[...])
    rows = to_places(slots_to_rows(terms, flat_ref))
    out_ref[pl.ds(0, senders, stride=2), :] = rows


def last_kernel(
    parts_ref, rows_ref, source_ref, relax_ref, window_ref, src_ref, fill_ref, multiplier_ref, grad_ref, flat_ref
):
    owners = rows_ref.shape[0] // 2
    rows = from_places(rows_ref[pl.ds(1, owners, stride=2), :])
    for j in range(8):
        flat_ref[pl.ds(j, owners, stride=8), :] = rows[:, WIDTH * j : WIDTH * (j + 1)]
    fetched = flat_ref[...].T
    relax = jnp.concatenate([relax_ref[...]] * 4, axis=0)
    multiplier = multiplier_of(parts_ref, source_ref, window_ref)
    for d in range(3):
        multiplier_ref[d] = multiplier[4 * d : 4 * d + 4]
    picked = select(relax * multiplier, src_ref[...])
    total = None
    for d in range(3):
        far = fetched[4 * d : 4 * d + 4]
        term = repeat_rows(picked, 4 * d, 1, 4) * jnp.concatenate([far] * 4, axis=0)
        total = term if total is None else total + term
    grad_ref[...] = total * live_row(fill_ref, src_ref.shape[1])


def call(kernel, out_shape, scratch, *operands, cost=None):
    return pl.pallas_call(
        kernel,
        out_shape=out_shape,
        in_specs=[pl.BlockSpec(memory_space=pltpu.VMEM)] * len(operands),
        scratch_shapes=scratch,
        compiler_params=pltpu.CompilerParams(vmem_limit_bytes=24 * MIB),
        cost_estimate=cost,
    )(*operands)


def exchange(rows):
    pools = lax.axis_size("pool")
    members = [(place + first_chip(pools)) % pools for place in range(pools)]
    members[:2] = members[1::-1]
    x = rows.reshape(pools, -1, 128)
    x = lax.all_to_all(x, "pool", 0, 0, axis_index_groups=[members], tiled=True)
    return x.reshape(rows.shape)


def share(part):
    groups = lax.axis_size("pb")
    members = [(place + groups // 2) % groups for place in range(groups)]
    return lax.all_to_all(part, "pb", 0, 0, axis_index_groups=[members], tiled=True)


def local(
    adjoint_source, deviation, relax_time, band_window, pair_src, pair_dst, bucket_fill, coupling
):
    states = band_window.shape[0]
    slots = pair_src.shape[0]
    pools = lax.axis_size("pool")
    window = band_window.reshape(1, states)
    src = pair_src.reshape(1, slots)
    dst = pair_dst.reshape(1, slots)
    sds = jax.ShapeDtypeStruct
    flat = pltpu.VMEM((slots, WIDTH), F32)
    partial = sds((lax.axis_size("pb"), 8, states * 3 // 2), F32)

    cost = pl.CostEstimate(flops=10**10, bytes_accessed=0, transcendentals=0)
    zero = call(zero_kernel, sds((8, 128), F32), [], cost=cost)
    sent = call(
        first_kernel, sds((pools, 128), F32), [flat],
        zero, coupling, adjoint_source, relax_time, window, src, dst, bucket_fill,
    )
    index = exchange(sent)
    gather = functools.partial(gather_kernel, states=states)
    parts = share(call(gather, partial, [], index, index))
    sent = call(
        second_kernel, sds((2 * pools, 128), F32), [flat],
        parts, index, deviation, adjoint_source, relax_time, window, src, bucket_fill, coupling,
    )
    rows = exchange(sent)
    parts = share(call(gather, partial, [], rows, index))
    return call(
        last_kernel, (sds(adjoint_source.shape, F32), sds(coupling.shape, F32)), [flat],
        parts, rows, adjoint_source, relax_time, window, src, bucket_fill,
    )


def solution(mesh):
    in_specs = (
        P(None, None, "pool"),
        P(None, None, "pool"),
        P(None, "pool"),
        P("pool"),
        P(("pool", "pb")),
        P(("pool", "pb")),
        P(("pool", "pb"), None),
        P(None, ("pool", "pb")),
    )
    out_specs = (P(None, None, "pool"), P(None, ("pool", "pb")))
    return jax.shard_map(local, mesh=mesh, in_specs=in_specs, out_specs=out_specs, check_vma=False)
```

```python
import functools

import jax
import jax.numpy as jnp
from jax import lax
from jax.experimental import pallas as pl
from jax.experimental.pallas import tpu as pltpu
from jax.sharding import PartitionSpec as P

ITERS = 2
WIDTH = 16
F32 = jnp.float32
BF16 = jnp.bfloat16
MIB = 1024 * 1024


def split3(x):
    high = x.astype(BF16)
    rest = x - high.astype(F32)
    middle = rest.astype(BF16)
    low = (rest - middle.astype(F32)).astype(BF16)
    return jnp.concatenate([high, middle, low], axis=0)


def tiles_of(x):
    parts = split3(x)
    width = min(128, x.shape[1])
    return jnp.concatenate([parts[:, t : t + width] for t in range(0, x.shape[1], width)], axis=0)


def whole(parts):
    return parts[:16] + parts[16:32] + parts[32:48]


def select(x, index):
    width = min(128, x.shape[1])
    rows = lax.broadcasted_iota(jnp.int32, (width, index.shape[1]), 0)
    hot = jnp.where(rows == (index & (width - 1)), 1.0, 0.0).astype(BF16)
    found = jnp.dot(tiles_of(x), hot, preferred_element_type=F32)
    at = jnp.broadcast_to(index, (16, index.shape[1])) >> (width.bit_length() - 1)
    total = whole(found[:48])
    for tile in range(1, x.shape[1] // width):
        total = jnp.where(at == tile, whole(found[48 * tile : 48 * tile + 48]), total)
    return total


def pick(x, index):
    parts = []
    width = min(128, index.shape[1])
    for first in range(0, index.shape[1], width):
        at = jnp.broadcast_to(index[:, first : first + width], (x.shape[0], width))
        part = jnp.zeros(at.shape, F32)
        for tile in range(x.shape[1] // 128):
            columns = x[:, 128 * tile : 128 * (tile + 1)]
            found = jnp.take_along_axis(columns, at & 127, axis=1, mode="promise_in_bounds")
            part = jnp.where(at >> 7 == tile, found, part)
        parts.append(part)
    return jnp.concatenate(parts, axis=1)


def rows16(ref):
    return jnp.concatenate([ref[0], ref[1], ref[2], jnp.zeros_like(ref[0])], axis=0)


def window16(window_ref):
    rows = lax.broadcasted_iota(jnp.int32, (16, window_ref.shape[1]), 0)
    return ((window_ref[...] >> (rows & 3)) & 1).astype(F32)


def live_row(fill_ref, slots):
    owners = fill_ref.shape[1]
    capacity = slots // owners
    fill = jnp.broadcast_to(fill_ref[...].astype(F32), (8, owners))
    lane = lax.broadcasted_iota(jnp.int32, (8, owners), 1)
    place = (lane & (capacity - 1)).astype(F32)
    parts = []
    for first in range(0, owners, owners // capacity):
        filled = jnp.take_along_axis(fill, first + (lane >> (capacity.bit_length() - 1)), axis=1, mode="promise_in_bounds")
        parts.append(jnp.where(place < filled, 1.0, 0.0)[:1])
    return jnp.concatenate(parts, axis=1)


def repeat_rows(x, first, step, count):
    row = lax.broadcasted_iota(jnp.int32, (16, x.shape[1]), 0)
    out = jnp.broadcast_to(x[first : first + 1], row.shape)
    for i in range(1, count):
        out = jnp.where(row >= 4 * i, x[first + step * i : first + step * i + 1], out)
    return out


def scatter_terms(picked, live, couple):
    total = None
    for band in range(4):
        block = couple[4 * band : 4 * band + 4]
        block = jnp.concatenate([block, block, block, jnp.zeros_like(block)], axis=0)
        term = block * repeat_rows(picked, band, 4, 3)
        total = term if total is None else total + term
    return total * live


def slots_to_rows(x, flat_ref):
    owners = x.shape[1] // 8
    flat_ref[...] = x.T
    return jnp.concatenate([flat_ref[pl.ds(j, owners, stride=8), :] for j in range(8)], axis=1)


def first_chip(pools):
    return pools * 9 // 16


def to_places(rows):
    start = first_chip(rows.shape[0])
    return jnp.concatenate([rows[start + 1 : start + 2], rows[start : start + 1], rows[start + 2 :], rows[:start]], axis=0)


def from_places(rows):
    rest = rows.shape[0] - first_chip(rows.shape[0])
    return jnp.concatenate([rows[rest:], rows[1:2], rows[:1], rows[2:rest]], axis=0)


def pack(x):
    half = x.shape[1] // 2
    tail = jnp.concatenate([x[8:12, :half], x[8:12, half:]], axis=0)
    return jnp.concatenate([x[:8], tail], axis=1)


def unpack(x):
    whole = x.shape[1] * 2 // 3
    tail = jnp.concatenate([x[:4, whole:], x[4:, whole:]], axis=1)
    return jnp.concatenate([x[:8, :whole], jnp.concatenate([tail, jnp.zeros_like(tail)], axis=0)], axis=0)


def received_slots(rows):
    turned = rows.T
    return jnp.concatenate([turned[WIDTH * j : WIDTH * (j + 1)] for j in range(8)], axis=1)


def received_hot(rows, states):
    width = min(256, states)
    lane = lax.broadcasted_iota(jnp.int32, (rows.shape[0], width), 1).astype(F32).astype(BF16)
    blocks = []
    for j in range(8):
        column = rows[:, WIDTH * j + 12 : WIDTH * j + 13]
        parts = [
            jnp.where((column - first).astype(BF16) == lane, jnp.ones_like(lane), jnp.zeros_like(lane))
            for first in range(0, states, width)
        ]
        blocks.append(jnp.concatenate(parts, axis=1))
    return jnp.concatenate(blocks, axis=0)


def zero_kernel(out_ref):
    out_ref[...] = jnp.zeros_like(out_ref)


def first_kernel(
    zero_ref, couple_ref, source_ref, relax_ref, window_ref, src_ref, dst_ref, fill_ref, out_ref, flat_ref
):
    live = live_row(fill_ref, src_ref.shape[1])
    relax = jnp.concatenate([relax_ref[...]] * 4, axis=0)
    moment = rows16(source_ref) * window16(window_ref) * relax
    terms = scatter_terms(pick(moment, src_ref[...]), live, couple_ref[...])
    row = lax.broadcasted_iota(jnp.int32, terms.shape, 0)
    terms = jnp.where(row == 12, dst_ref[...].astype(F32) + zero_ref[:1, :1], terms)
    out_ref[...] = to_places(slots_to_rows(terms, flat_ref))


def gather_kernel(rows_ref, index_ref, out_ref, *, states):
    senders = index_ref.shape[0]
    depth = rows_ref.shape[0] // senders
    rows = rows_ref[...] if depth == 1 else rows_ref[pl.ds(0, senders, stride=depth), :]
    hot = received_hot(index_ref[...], states)
    packed = pack(whole(jnp.dot(split3(received_slots(rows)), hot, preferred_element_type=F32)))
    for i in range(out_ref.shape[0]):
        out_ref[i] = packed


def returned_rows(dev_ref, window_ref, index_ref):
    masked = rows16(dev_ref) * window16(window_ref)
    turned = index_ref[...].T.astype(jnp.int32)
    found = [pick(masked, turned[WIDTH * j + 12 : WIDTH * j + 13]) for j in range(8)]
    return jnp.concatenate(found, axis=0).T


def multiplier_of(part, source_ref, window_ref):
    window = window16(window_ref)
    return window * (rows16(source_ref) + unpack((part[0] + part[1]) + (part[2] + part[3])))


def second_kernel(
    parts_ref, index_ref, dev_ref, source_ref, relax_ref, window_ref, src_ref, fill_ref, couple_ref, out_ref, flat_ref
):
    senders = index_ref.shape[0]
    out_ref[pl.ds(1, senders, stride=2), :] = returned_rows(dev_ref, window_ref, index_ref)
    relax = jnp.concatenate([relax_ref[...]] * 4, axis=0)
    moment = relax * multiplier_of(parts_ref, source_ref, window_ref)
    live = live_row(fill_ref, src_ref.shape[1])
    terms = scatter_terms(select(moment, src_ref[...]), live, couple_ref[...])
    rows = to_places(slots_to_rows(terms, flat_ref))
    out_ref[pl.ds(0, senders, stride=2), :] = rows


def last_kernel(
    parts_ref, rows_ref, source_ref, relax_ref, window_ref, src_ref, fill_ref, multiplier_ref, grad_ref, flat_ref
):
    owners = rows_ref.shape[0] // 2
    rows = from_places(rows_ref[pl.ds(1, owners, stride=2), :])
    for j in range(8):
        flat_ref[pl.ds(j, owners, stride=8), :] = rows[:, WIDTH * j : WIDTH * (j + 1)]
    fetched = flat_ref[...].T
    relax = jnp.concatenate([relax_ref[...]] * 4, axis=0)
    multiplier = multiplier_of(parts_ref, source_ref, window_ref)
    for d in range(3):
        multiplier_ref[d] = multiplier[4 * d : 4 * d + 4]
    picked = select(relax * multiplier, src_ref[...])
    total = None
    for d in range(3):
        far = fetched[4 * d : 4 * d + 4]
        term = repeat_rows(picked, 4 * d, 1, 4) * jnp.concatenate([far] * 4, axis=0)
        total = term if total is None else total + term
    grad_ref[...] = total * live_row(fill_ref, src_ref.shape[1])


def call(kernel, out_shape, scratch, *operands, cost=None):
    return pl.pallas_call(
        kernel,
        out_shape=out_shape,
        in_specs=[pl.BlockSpec(memory_space=pltpu.VMEM)] * len(operands),
        scratch_shapes=scratch,
        compiler_params=pltpu.CompilerParams(vmem_limit_bytes=24 * MIB),
        cost_estimate=cost,
    )(*operands)


def exchange(rows):
    pools = lax.axis_size("pool")
    members = [(place + first_chip(pools)) % pools for place in range(pools)]
    members[:2] = members[1::-1]
    x = rows.reshape(pools, -1, 128)
    x = lax.all_to_all(x, "pool", 0, 0, axis_index_groups=[members], tiled=True)
    return x.reshape(rows.shape)


def share(part):
    groups = lax.axis_size("pb")
    members = [(place + groups // 2) % groups for place in range(groups)]
    return lax.all_to_all(part, "pb", 0, 0, axis_index_groups=[members], tiled=True)


def local(
    adjoint_source, deviation, relax_time, band_window, pair_src, pair_dst, bucket_fill, coupling
):
    states = band_window.shape[0]
    slots = pair_src.shape[0]
    pools = lax.axis_size("pool")
    window = band_window.reshape(1, states)
    src = pair_src.reshape(1, slots)
    dst = pair_dst.reshape(1, slots)
    sds = jax.ShapeDtypeStruct
    flat = pltpu.VMEM((slots, WIDTH), F32)
    partial = sds((lax.axis_size("pb"), 8, states * 3 // 2), F32)

    cost = pl.CostEstimate(flops=10**10, bytes_accessed=0, transcendentals=0)
    zero = call(zero_kernel, sds((8, 128), F32), [], cost=cost)
    sent = call(
        first_kernel, sds((pools, 128), F32), [flat],
        zero, coupling, adjoint_source, relax_time, window, src, dst, bucket_fill,
    )
    index = exchange(sent)
    gather = functools.partial(gather_kernel, states=states)
    parts = share(call(gather, partial, [], index, index))
    sent = call(
        second_kernel, sds((2 * pools, 128), F32), [flat],
        parts, index, deviation, adjoint_source, relax_time, window, src, bucket_fill, coupling,
    )
    rows = exchange(sent)
    parts = share(call(gather, partial, [], rows, index))
    return call(
        last_kernel, (sds(adjoint_source.shape, F32), sds(coupling.shape, F32)), [flat],
        parts, rows, adjoint_source, relax_time, window, src, bucket_fill,
    )


def solution(mesh):
    in_specs = (
        P(None, None, "pool"),
        P(None, None, "pool"),
        P(None, "pool"),
        P("pool"),
        P(("pool", "pb")),
        P(("pool", "pb")),
        P(("pool", "pb"), None),
        P(None, ("pool", "pb")),
    )
    out_specs = (P(None, None, "pool"), P(None, ("pool", "pb")))
    return jax.shard_map(local, mesh=mesh, in_specs=in_specs, out_specs=out_specs, check_vma=False)
```

```python
import functools

import jax
import jax.numpy as jnp
from jax import lax
from jax.experimental import pallas as pl
from jax.experimental.pallas import tpu as pltpu
from jax.sharding import PartitionSpec as P

ITERS = 2
WIDTH = 16
F32 = jnp.float32
BF16 = jnp.bfloat16
MIB = 1024 * 1024


def split3(x):
    high = x.astype(BF16)
    rest = x - high.astype(F32)
    middle = rest.astype(BF16)
    low = (rest - middle.astype(F32)).astype(BF16)
    return jnp.concatenate([high, middle, low], axis=0)


def tiles_of(x):
    parts = split3(x)
    width = min(128, x.shape[1])
    return jnp.concatenate([parts[:, t : t + width] for t in range(0, x.shape[1], width)], axis=0)


def whole(parts):
    return parts[:16] + parts[16:32] + parts[32:48]


def select(x, index):
    width = min(128, x.shape[1])
    rows = lax.broadcasted_iota(jnp.int32, (width, index.shape[1]), 0)
    hot = jnp.where(rows == (index & (width - 1)), 1.0, 0.0).astype(BF16)
    found = jnp.dot(tiles_of(x), hot, preferred_element_type=F32)
    at = jnp.broadcast_to(index, (16, index.shape[1])) >> (width.bit_length() - 1)
    total = whole(found[:48])
    for tile in range(1, x.shape[1] // width):
        total = jnp.where(at == tile, whole(found[48 * tile : 48 * tile + 48]), total)
    return total


def pick(x, index):
    parts = []
    width = min(128, index.shape[1])
    for first in range(0, index.shape[1], width):
        at = jnp.broadcast_to(index[:, first : first + width], (x.shape[0], width))
        part = jnp.zeros(at.shape, F32)
        for tile in range(x.shape[1] // 128):
            columns = x[:, 128 * tile : 128 * (tile + 1)]
            found = jnp.take_along_axis(columns, at & 127, axis=1, mode="promise_in_bounds")
            part = jnp.where(at >> 7 == tile, found, part)
        parts.append(part)
    return jnp.concatenate(parts, axis=1)


def rows16(ref):
    return jnp.concatenate([ref[0], ref[1], ref[2], jnp.zeros_like(ref[0])], axis=0)


def window16(window_ref):
    rows = lax.broadcasted_iota(jnp.int32, (16, window_ref.shape[1]), 0)
    return ((window_ref[...] >> (rows & 3)) & 1).astype(F32)


def live_row(fill_ref, slots):
    owners = fill_ref.shape[1]
    capacity = slots // owners
    fill = jnp.broadcast_to(fill_ref[...].astype(F32), (8, owners))
    lane = lax.broadcasted_iota(jnp.int32, (8, owners), 1)
    place = (lane & (capacity - 1)).astype(F32)
    parts = []
    for first in range(0, owners, owners // capacity):
        filled = jnp.take_along_axis(fill, first + (lane >> (capacity.bit_length() - 1)), axis=1, mode="promise_in_bounds")
        parts.append(jnp.where(place < filled, 1.0, 0.0)[:1])
    return jnp.concatenate(parts, axis=1)


def repeat_rows(x, first, step, count):
    row = lax.broadcasted_iota(jnp.int32, (16, x.shape[1]), 0)
    out = jnp.broadcast_to(x[first : first + 1], row.shape)
    for i in range(1, count):
        out = jnp.where(row >= 4 * i, x[first + step * i : first + step * i + 1], out)
    return out


def scatter_terms(picked, live, couple):
    total = None
    for band in range(4):
        block = couple[4 * band : 4 * band + 4]
        block = jnp.concatenate([block, block, block, jnp.zeros_like(block)], axis=0)
        term = block * repeat_rows(picked, band, 4, 3)
        total = term if total is None else total + term
    return total * live


def slots_to_rows(x, flat_ref):
    owners = x.shape[1] // 8
    flat_ref[...] = x.T
    return jnp.concatenate([flat_ref[pl.ds(j, owners, stride=8), :] for j in range(8)], axis=1)


def first_chip(pools):
    return pools * 11 // 16


def to_places(rows):
    start = first_chip(rows.shape[0])
    return jnp.concatenate([rows[start + 1 : start + 2], rows[start : start + 1], rows[start + 2 :], rows[:start]], axis=0)


def from_places(rows):
    rest = rows.shape[0] - first_chip(rows.shape[0])
    return jnp.concatenate([rows[rest:], rows[1:2], rows[:1], rows[2:rest]], axis=0)


def pack(x):
    half = x.shape[1] // 2
    tail = jnp.concatenate([x[8:12, :half], x[8:12, half:]], axis=0)
    return jnp.concatenate([x[:8], tail], axis=1)


def unpack(x):
    whole = x.shape[1] * 2 // 3
    tail = jnp.concatenate([x[:4, whole:], x[4:, whole:]], axis=1)
    return jnp.concatenate([x[:8, :whole], jnp.concatenate([tail, jnp.zeros_like(tail)], axis=0)], axis=0)


def received_slots(rows):
    turned = rows.T
    return jnp.concatenate([turned[WIDTH * j : WIDTH * (j + 1)] for j in range(8)], axis=1)


def received_hot(rows, states):
    width = min(256, states)
    lane = lax.broadcasted_iota(jnp.int32, (rows.shape[0], width), 1).astype(F32).astype(BF16)
    blocks = []
    for j in range(8):
        column = rows[:, WIDTH * j + 12 : WIDTH * j + 13]
        parts = [
            jnp.where((column - first).astype(BF16) == lane, jnp.ones_like(lane), jnp.zeros_like(lane))
            for first in range(0, states, width)
        ]
        blocks.append(jnp.concatenate(parts, axis=1))
    return jnp.concatenate(blocks, axis=0)


def zero_kernel(out_ref):
    out_ref[...] = jnp.zeros_like(out_ref)


def first_kernel(
    zero_ref, couple_ref, source_ref, relax_ref, window_ref, src_ref, dst_ref, fill_ref, out_ref, flat_ref
):
    live = live_row(fill_ref, src_ref.shape[1])
    relax = jnp.concatenate([relax_ref[...]] * 4, axis=0)
    moment = rows16(source_ref) * window16(window_ref) * relax
    terms = scatter_terms(pick(moment, src_ref[...]), live, couple_ref[...])
    row = lax.broadcasted_iota(jnp.int32, terms.shape, 0)
    terms = jnp.where(row == 12, dst_ref[...].astype(F32) + zero_ref[:1, :1], terms)
    out_ref[...] = to_places(slots_to_rows(terms, flat_ref))


def gather_kernel(rows_ref, index_ref, out_ref, *, states):
    senders = index_ref.shape[0]
    depth = rows_ref.shape[0] // senders
    rows = rows_ref[...] if depth == 1 else rows_ref[pl.ds(0, senders, stride=depth), :]
    hot = received_hot(index_ref[...], states)
    packed = pack(whole(jnp.dot(split3(received_slots(rows)), hot, preferred_element_type=F32)))
    for i in range(out_ref.shape[0]):
        out_ref[i] = packed


def returned_rows(dev_ref, window_ref, index_ref):
    masked = rows16(dev_ref) * window16(window_ref)
    turned = index_ref[...].T.astype(jnp.int32)
    found = [pick(masked, turned[WIDTH * j + 12 : WIDTH * j + 13]) for j in range(8)]
    return jnp.concatenate(found, axis=0).T


def multiplier_of(part, source_ref, window_ref):
    window = window16(window_ref)
    return window * (rows16(source_ref) + unpack((part[0] + part[1]) + (part[2] + part[3])))


def second_kernel(
    parts_ref, index_ref, dev_ref, source_ref, relax_ref, window_ref, src_ref, fill_ref, couple_ref, out_ref, flat_ref
):
    senders = index_ref.shape[0]
    out_ref[pl.ds(1, senders, stride=2), :] = returned_rows(dev_ref, window_ref, index_ref)
    relax = jnp.concatenate([relax_ref[...]] * 4, axis=0)
    moment = relax * multiplier_of(parts_ref, source_ref, window_ref)
    live = live_row(fill_ref, src_ref.shape[1])
    terms = scatter_terms(select(moment, src_ref[...]), live, couple_ref[...])
    rows = to_places(slots_to_rows(terms, flat_ref))
    out_ref[pl.ds(0, senders, stride=2), :] = rows


def last_kernel(
    parts_ref, rows_ref, source_ref, relax_ref, window_ref, src_ref, fill_ref, multiplier_ref, grad_ref, flat_ref
):
    owners = rows_ref.shape[0] // 2
    rows = from_places(rows_ref[pl.ds(1, owners, stride=2), :])
    for j in range(8):
        flat_ref[pl.ds(j, owners, stride=8), :] = rows[:, WIDTH * j : WIDTH * (j + 1)]
    fetched = flat_ref[...].T
    relax = jnp.concatenate([relax_ref[...]] * 4, axis=0)
    multiplier = multiplier_of(parts_ref, source_ref, window_ref)
    for d in range(3):
        multiplier_ref[d] = multiplier[4 * d : 4 * d + 4]
    picked = select(relax * multiplier, src_ref[...])
    total = None
    for d in range(3):
        far = fetched[4 * d : 4 * d + 4]
        term = repeat_rows(picked, 4 * d, 1, 4) * jnp.concatenate([far] * 4, axis=0)
        total = term if total is None else total + term
    grad_ref[...] = total * live_row(fill_ref, src_ref.shape[1])


def call(kernel, out_shape, scratch, *operands, cost=None):
    return pl.pallas_call(
        kernel,
        out_shape=out_shape,
        in_specs=[pl.BlockSpec(memory_space=pltpu.VMEM)] * len(operands),
        scratch_shapes=scratch,
        compiler_params=pltpu.CompilerParams(vmem_limit_bytes=24 * MIB),
        cost_estimate=cost,
    )(*operands)


def exchange(rows):
    pools = lax.axis_size("pool")
    members = [(place + first_chip(pools)) % pools for place in range(pools)]
    members[:2] = members[1::-1]
    x = rows.reshape(pools, -1, 128)
    x = lax.all_to_all(x, "pool", 0, 0, axis_index_groups=[members], tiled=True)
    return x.reshape(rows.shape)


def share(part, first):
    groups = lax.axis_size("pb")
    members = [(place + first) % groups for place in range(groups)]
    return lax.all_to_all(part, "pb", 0, 0, axis_index_groups=[members], tiled=True)


def local(
    adjoint_source, deviation, relax_time, band_window, pair_src, pair_dst, bucket_fill, coupling
):
    states = band_window.shape[0]
    slots = pair_src.shape[0]
    pools = lax.axis_size("pool")
    window = band_window.reshape(1, states)
    src = pair_src.reshape(1, slots)
    dst = pair_dst.reshape(1, slots)
    sds = jax.ShapeDtypeStruct
    flat = pltpu.VMEM((slots, WIDTH), F32)
    partial = sds((lax.axis_size("pb"), 8, states * 3 // 2), F32)

    cost = pl.CostEstimate(flops=10**10, bytes_accessed=0, transcendentals=0)
    zero = call(zero_kernel, sds((8, 128), F32), [], cost=cost)
    sent = call(
        first_kernel, sds((pools, 128), F32), [flat],
        zero, coupling, adjoint_source, relax_time, window, src, dst, bucket_fill,
    )
    index = exchange(sent)
    gather = functools.partial(gather_kernel, states=states)
    parts = share(call(gather, partial, [], index, index), 2)
    sent = call(
        second_kernel, sds((2 * pools, 128), F32), [flat],
        parts, index, deviation, adjoint_source, relax_time, window, src, bucket_fill, coupling,
    )
    rows = exchange(sent)
    parts = share(call(gather, partial, [], rows, index), 0)
    return call(
        last_kernel, (sds(adjoint_source.shape, F32), sds(coupling.shape, F32)), [flat],
        parts, rows, adjoint_source, relax_time, window, src, bucket_fill,
    )


def solution(mesh):
    in_specs = (
        P(None, None, "pool"),
        P(None, None, "pool"),
        P(None, "pool"),
        P("pool"),
        P(("pool", "pb")),
        P(("pool", "pb")),
        P(("pool", "pb"), None),
        P(None, ("pool", "pb")),
    )
    out_specs = (P(None, None, "pool"), P(None, ("pool", "pb")))
    return jax.shard_map(local, mesh=mesh, in_specs=in_specs, out_specs=out_specs, check_vma=False)
```

```python
import functools

import jax
import jax.numpy as jnp
from jax import lax
from jax.experimental import pallas as pl
from jax.experimental.pallas import tpu as pltpu
from jax.sharding import PartitionSpec as P

ITERS = 2
WIDTH = 16
F32 = jnp.float32
BF16 = jnp.bfloat16
MIB = 1024 * 1024


def split3(x):
    high = x.astype(BF16)
    rest = x - high.astype(F32)
    middle = rest.astype(BF16)
    low = (rest - middle.astype(F32)).astype(BF16)
    return jnp.concatenate([high, middle, low], axis=0)


def tiles_of(x):
    parts = split3(x)
    width = min(128, x.shape[1])
    return jnp.concatenate([parts[:, t : t + width] for t in range(0, x.shape[1], width)], axis=0)


def whole(parts):
    return parts[:16] + parts[16:32] + parts[32:48]


def select(x, index):
    width = min(128, x.shape[1])
    rows = lax.broadcasted_iota(jnp.int32, (width, index.shape[1]), 0)
    hot = jnp.where(rows == (index & (width - 1)), 1.0, 0.0).astype(BF16)
    found = jnp.dot(tiles_of(x), hot, preferred_element_type=F32)
    at = jnp.broadcast_to(index, (16, index.shape[1])) >> (width.bit_length() - 1)
    total = whole(found[:48])
    for tile in range(1, x.shape[1] // width):
        total = jnp.where(at == tile, whole(found[48 * tile : 48 * tile + 48]), total)
    return total


def pick(x, index):
    parts = []
    width = min(128, index.shape[1])
    for first in range(0, index.shape[1], width):
        at = jnp.broadcast_to(index[:, first : first + width], (x.shape[0], width))
        part = jnp.zeros(at.shape, F32)
        for tile in range(x.shape[1] // 128):
            columns = x[:, 128 * tile : 128 * (tile + 1)]
            found = jnp.take_along_axis(columns, at & 127, axis=1, mode="promise_in_bounds")
            part = jnp.where(at >> 7 == tile, found, part)
        parts.append(part)
    return jnp.concatenate(parts, axis=1)


def rows16(ref):
    return jnp.concatenate([ref[0], ref[1], ref[2], jnp.zeros_like(ref[0])], axis=0)


def window16(window_ref):
    rows = lax.broadcasted_iota(jnp.int32, (16, window_ref.shape[1]), 0)
    return ((window_ref[...] >> (rows & 3)) & 1).astype(F32)


def live_row(fill_ref, slots):
    owners = fill_ref.shape[1]
    capacity = slots // owners
    fill = jnp.broadcast_to(fill_ref[...].astype(F32), (8, owners))
    lane = lax.broadcasted_iota(jnp.int32, (8, owners), 1)
    place = (lane & (capacity - 1)).astype(F32)
    parts = []
    for first in range(0, owners, owners // capacity):
        filled = jnp.take_along_axis(fill, first + (lane >> (capacity.bit_length() - 1)), axis=1, mode="promise_in_bounds")
        parts.append(jnp.where(place < filled, 1.0, 0.0)[:1])
    return jnp.concatenate(parts, axis=1)


def repeat_rows(x, first, step, count):
    row = lax.broadcasted_iota(jnp.int32, (16, x.shape[1]), 0)
    out = jnp.broadcast_to(x[first : first + 1], row.shape)
    for i in range(1, count):
        out = jnp.where(row >= 4 * i, x[first + step * i : first + step * i + 1], out)
    return out


def scatter_terms(picked, live, couple):
    total = None
    for band in range(4):
        block = couple[4 * band : 4 * band + 4]
        block = jnp.concatenate([block, block, block, jnp.zeros_like(block)], axis=0)
        term = block * repeat_rows(picked, band, 4, 3)
        total = term if total is None else total + term
    return total * live


def slots_to_rows(x, flat_ref):
    owners = x.shape[1] // 8
    flat_ref[...] = x.T
    return jnp.concatenate([flat_ref[pl.ds(j, owners, stride=8), :] for j in range(8)], axis=1)


def first_chip(pools):
    return pools * 13 // 16


def to_places(rows):
    start = first_chip(rows.shape[0])
    return jnp.concatenate([rows[start + 1 : start + 2], rows[start : start + 1], rows[start + 2 :], rows[:start]], axis=0)


def from_places(rows):
    rest = rows.shape[0] - first_chip(rows.shape[0])
    return jnp.concatenate([rows[rest:], rows[1:2], rows[:1], rows[2:rest]], axis=0)


def pack(x):
    half = x.shape[1] // 2
    tail = jnp.concatenate([x[8:12, :half], x[8:12, half:]], axis=0)
    return jnp.concatenate([x[:8], tail], axis=1)


def unpack(x):
    whole = x.shape[1] * 2 // 3
    tail = jnp.concatenate([x[:4, whole:], x[4:, whole:]], axis=1)
    return jnp.concatenate([x[:8, :whole], jnp.concatenate([tail, jnp.zeros_like(tail)], axis=0)], axis=0)


def received_slots(rows):
    turned = rows.T
    return jnp.concatenate([turned[WIDTH * j : WIDTH * (j + 1)] for j in range(8)], axis=1)


def received_hot(rows, states):
    width = min(256, states)
    lane = lax.broadcasted_iota(jnp.int32, (rows.shape[0], width), 1).astype(F32).astype(BF16)
    blocks = []
    for j in range(8):
        column = rows[:, WIDTH * j + 12 : WIDTH * j + 13]
        parts = [
            jnp.where((column - first).astype(BF16) == lane, jnp.ones_like(lane), jnp.zeros_like(lane))
            for first in range(0, states, width)
        ]
        blocks.append(jnp.concatenate(parts, axis=1))
    return jnp.concatenate(blocks, axis=0)


def zero_kernel(out_ref):
    out_ref[...] = jnp.zeros_like(out_ref)


def first_kernel(
    zero_ref, couple_ref, source_ref, relax_ref, window_ref, src_ref, dst_ref, fill_ref, out_ref, live_ref, flat_ref
):
    live = live_row(fill_ref, src_ref.shape[1])
    live_ref[...] = live
    relax = jnp.concatenate([relax_ref[...]] * 4, axis=0)
    moment = rows16(source_ref) * window16(window_ref) * relax
    terms = scatter_terms(pick(moment, src_ref[...]), live, couple_ref[...])
    row = lax.broadcasted_iota(jnp.int32, terms.shape, 0)
    terms = jnp.where(row == 12, dst_ref[...].astype(F32) + zero_ref[:1, :1], terms)
    out_ref[...] = to_places(slots_to_rows(terms, flat_ref))


def gather_kernel(rows_ref, index_ref, out_ref, *, states):
    senders = index_ref.shape[0]
    depth = rows_ref.shape[0] // senders
    rows = rows_ref[...] if depth == 1 else rows_ref[pl.ds(0, senders, stride=depth), :]
    hot = received_hot(index_ref[...], states)
    packed = pack(whole(jnp.dot(split3(received_slots(rows)), hot, preferred_element_type=F32)))
    for i in range(out_ref.shape[0]):
        out_ref[i] = packed


def returned_rows(dev_ref, window_ref, index_ref):
    masked = rows16(dev_ref) * window16(window_ref)
    turned = index_ref[...].T.astype(jnp.int32)
    found = [pick(masked, turned[WIDTH * j + 12 : WIDTH * j + 13]) for j in range(8)]
    return jnp.concatenate(found, axis=0).T


def multiplier_of(part, source_ref, window_ref):
    window = window16(window_ref)
    return window * (rows16(source_ref) + unpack((part[0] + part[1]) + (part[2] + part[3])))


def second_kernel(
    parts_ref, index_ref, dev_ref, source_ref, relax_ref, window_ref, src_ref, live_ref, couple_ref, out_ref, flat_ref
):
    senders = index_ref.shape[0]
    out_ref[pl.ds(1, senders, stride=2), :] = returned_rows(dev_ref, window_ref, index_ref)
    relax = jnp.concatenate([relax_ref[...]] * 4, axis=0)
    moment = relax * multiplier_of(parts_ref, source_ref, window_ref)
    terms = scatter_terms(select(moment, src_ref[...]), live_ref[...], couple_ref[...])
    rows = to_places(slots_to_rows(terms, flat_ref))
    out_ref[pl.ds(0, senders, stride=2), :] = rows


def last_kernel(
    parts_ref, rows_ref, source_ref, relax_ref, window_ref, src_ref, live_ref, multiplier_ref, grad_ref, flat_ref
):
    owners = rows_ref.shape[0] // 2
    rows = from_places(rows_ref[pl.ds(1, owners, stride=2), :])
    for j in range(8):
        flat_ref[pl.ds(j, owners, stride=8), :] = rows[:, WIDTH * j : WIDTH * (j + 1)]
    fetched = flat_ref[...].T
    relax = jnp.concatenate([relax_ref[...]] * 4, axis=0)
    multiplier = multiplier_of(parts_ref, source_ref, window_ref)
    for d in range(3):
        multiplier_ref[d] = multiplier[4 * d : 4 * d + 4]
    picked = select(relax * multiplier, src_ref[...])
    total = None
    for d in range(3):
        far = fetched[4 * d : 4 * d + 4]
        term = repeat_rows(picked, 4 * d, 1, 4) * jnp.concatenate([far] * 4, axis=0)
        total = term if total is None else total + term
    grad_ref[...] = total * live_ref[...]


def call(kernel, out_shape, scratch, *operands, cost=None):
    return pl.pallas_call(
        kernel,
        out_shape=out_shape,
        in_specs=[pl.BlockSpec(memory_space=pltpu.VMEM)] * len(operands),
        scratch_shapes=scratch,
        compiler_params=pltpu.CompilerParams(vmem_limit_bytes=24 * MIB),
        cost_estimate=cost,
    )(*operands)


def exchange(rows):
    pools = lax.axis_size("pool")
    members = [(place + first_chip(pools)) % pools for place in range(pools)]
    members[:2] = members[1::-1]
    x = rows.reshape(pools, -1, 128)
    x = lax.all_to_all(x, "pool", 0, 0, axis_index_groups=[members], tiled=True)
    return x.reshape(rows.shape)


def share(part):
    groups = lax.axis_size("pb")
    members = [(place + groups // 2) % groups for place in range(groups)]
    return lax.all_to_all(part, "pb", 0, 0, axis_index_groups=[members], tiled=True)


def local(
    adjoint_source, deviation, relax_time, band_window, pair_src, pair_dst, bucket_fill, coupling
):
    states = band_window.shape[0]
    slots = pair_src.shape[0]
    pools = lax.axis_size("pool")
    window = band_window.reshape(1, states)
    src = pair_src.reshape(1, slots)
    dst = pair_dst.reshape(1, slots)
    sds = jax.ShapeDtypeStruct
    flat = pltpu.VMEM((slots, WIDTH), F32)
    partial = sds((lax.axis_size("pb"), 8, states * 3 // 2), F32)

    cost = pl.CostEstimate(flops=10**10, bytes_accessed=0, transcendentals=0)
    zero = call(zero_kernel, sds((8, 128), F32), [], cost=cost)
    sent, live = call(
        first_kernel, (sds((pools, 128), F32), sds((1, slots), F32)), [flat],
        zero, coupling, adjoint_source, relax_time, window, src, dst, bucket_fill,
    )
    index = exchange(sent)
    gather = functools.partial(gather_kernel, states=states)
    parts = share(call(gather, partial, [], index, index))
    sent = call(
        second_kernel, sds((2 * pools, 128), F32), [flat],
        parts, index, deviation, adjoint_source, relax_time, window, src, live, coupling,
    )
    rows = exchange(sent)
    parts = share(call(gather, partial, [], rows, index))
    return call(
        last_kernel, (sds(adjoint_source.shape, F32), sds(coupling.shape, F32)), [flat],
        parts, rows, adjoint_source, relax_time, window, src, live,
    )


def solution(mesh):
    in_specs = (
        P(None, None, "pool"),
        P(None, None, "pool"),
        P(None, "pool"),
        P("pool"),
        P(("pool", "pb")),
        P(("pool", "pb")),
        P(("pool", "pb"), None),
        P(None, ("pool", "pb")),
    )
    out_specs = (P(None, None, "pool"), P(None, ("pool", "pb")))
    return jax.shard_map(local, mesh=mesh, in_specs=in_specs, out_specs=out_specs, check_vma=False)
```

```python
import functools

import jax
import jax.numpy as jnp
from jax import lax
from jax.experimental import pallas as pl
from jax.experimental.pallas import tpu as pltpu
from jax.sharding import PartitionSpec as P

ITERS = 2
WIDTH = 16
F32 = jnp.float32
BF16 = jnp.bfloat16
MIB = 1024 * 1024


def split3(x):
    high = x.astype(BF16)
    rest = x - high.astype(F32)
    middle = rest.astype(BF16)
    low = (rest - middle.astype(F32)).astype(BF16)
    return jnp.concatenate([high, middle, low], axis=0)


def tiles_of(x):
    parts = split3(x)
    width = min(128, x.shape[1])
    return jnp.concatenate([parts[:, t : t + width] for t in range(0, x.shape[1], width)], axis=0)


def whole(parts):
    return parts[:16] + parts[16:32] + parts[32:48]


def select(x, index):
    width = min(128, x.shape[1])
    rows = lax.broadcasted_iota(jnp.int32, (width, index.shape[1]), 0)
    hot = jnp.where(rows == (index & (width - 1)), 1.0, 0.0).astype(BF16)
    found = jnp.dot(tiles_of(x), hot, preferred_element_type=F32)
    at = jnp.broadcast_to(index, (16, index.shape[1])) >> (width.bit_length() - 1)
    total = whole(found[:48])
    for tile in range(1, x.shape[1] // width):
        total = jnp.where(at == tile, whole(found[48 * tile : 48 * tile + 48]), total)
    return total


def pick(x, index):
    parts = []
    width = min(128, index.shape[1])
    for first in range(0, index.shape[1], width):
        at = jnp.broadcast_to(index[:, first : first + width], (x.shape[0], width))
        part = jnp.zeros(at.shape, F32)
        for tile in range(x.shape[1] // 128):
            columns = x[:, 128 * tile : 128 * (tile + 1)]
            found = jnp.take_along_axis(columns, at & 127, axis=1, mode="promise_in_bounds")
            part = jnp.where(at >> 7 == tile, found, part)
        parts.append(part)
    return jnp.concatenate(parts, axis=1)


def rows16(ref):
    return jnp.concatenate([ref[0], ref[1], ref[2], jnp.zeros_like(ref[0])], axis=0)


def window16(window_ref):
    rows = lax.broadcasted_iota(jnp.int32, (16, window_ref.shape[1]), 0)
    return ((window_ref[...] >> (rows & 3)) & 1).astype(F32)


def live_row(fill_ref, slots):
    owners = fill_ref.shape[1]
    capacity = slots // owners
    fill = jnp.broadcast_to(fill_ref[...].astype(F32), (8, owners))
    lane = lax.broadcasted_iota(jnp.int32, (8, owners), 1)
    place = (lane & (capacity - 1)).astype(F32)
    parts = []
    for first in range(0, owners, owners // capacity):
        filled = jnp.take_along_axis(fill, first + (lane >> (capacity.bit_length() - 1)), axis=1, mode="promise_in_bounds")
        parts.append(jnp.where(place < filled, 1.0, 0.0)[:1])
    return jnp.concatenate(parts, axis=1)


def repeat_rows(x, first, step, count):
    row = lax.broadcasted_iota(jnp.int32, (16, x.shape[1]), 0)
    out = jnp.broadcast_to(x[first : first + 1], row.shape)
    for i in range(1, count):
        out = jnp.where(row >= 4 * i, x[first + step * i : first + step * i + 1], out)
    return out


def scatter_terms(picked, live, couple):
    total = None
    for band in range(4):
        block = couple[4 * band : 4 * band + 4]
        block = jnp.concatenate([block, block, block, jnp.zeros_like(block)], axis=0)
        term = block * repeat_rows(picked, band, 4, 3)
        total = term if total is None else total + term
    return total * live


def slots_to_rows(x, flat_ref):
    owners = x.shape[1] // 8
    flat_ref[...] = x.T
    return jnp.concatenate([flat_ref[pl.ds(j, owners, stride=8), :] for j in range(8)], axis=1)


def first_chip(pools):
    return pools * 51 // 64


def to_places(rows):
    start = first_chip(rows.shape[0])
    return jnp.concatenate([rows[start + 1 : start + 2], rows[start : start + 1], rows[start + 2 :], rows[:start]], axis=0)


def from_places(rows):
    rest = rows.shape[0] - first_chip(rows.shape[0])
    return jnp.concatenate([rows[rest:], rows[1:2], rows[:1], rows[2:rest]], axis=0)


def pack(x):
    half = x.shape[1] // 2
    tail = jnp.concatenate([x[8:12, :half], x[8:12, half:]], axis=0)
    return jnp.concatenate([x[:8], tail], axis=1)


def unpack(x):
    whole = x.shape[1] * 2 // 3
    tail = jnp.concatenate([x[:4, whole:], x[4:, whole:]], axis=1)
    return jnp.concatenate([x[:8, :whole], jnp.concatenate([tail, jnp.zeros_like(tail)], axis=0)], axis=0)


def received_slots(rows):
    turned = rows.T
    return jnp.concatenate([turned[WIDTH * j : WIDTH * (j + 1)] for j in range(8)], axis=1)


def received_hot(rows, states):
    width = min(256, states)
    lane = lax.broadcasted_iota(jnp.int32, (rows.shape[0], width), 1).astype(F32).astype(BF16)
    blocks = []
    for j in range(8):
        column = rows[:, WIDTH * j + 12 : WIDTH * j + 13]
        parts = [
            jnp.where((column - first).astype(BF16) == lane, jnp.ones_like(lane), jnp.zeros_like(lane))
            for first in range(0, states, width)
        ]
        blocks.append(jnp.concatenate(parts, axis=1))
    return jnp.concatenate(blocks, axis=0)


def zero_kernel(out_ref):
    out_ref[...] = jnp.zeros_like(out_ref)


def first_kernel(
    zero_ref, couple_ref, source_ref, relax_ref, window_ref, src_ref, dst_ref, fill_ref, out_ref, live_ref, flat_ref
):
    live = live_row(fill_ref, src_ref.shape[1])
    live_ref[...] = live
    relax = jnp.concatenate([relax_ref[...]] * 4, axis=0)
    moment = rows16(source_ref) * window16(window_ref) * relax
    terms = scatter_terms(pick(moment, src_ref[...]), live, couple_ref[...])
    row = lax.broadcasted_iota(jnp.int32, terms.shape, 0)
    terms = jnp.where(row == 12, dst_ref[...].astype(F32) + zero_ref[:1, :1], terms)
    out_ref[...] = to_places(slots_to_rows(terms, flat_ref))


def gather_kernel(rows_ref, index_ref, out_ref, *, states):
    senders = index_ref.shape[0]
    depth = rows_ref.shape[0] // senders
    rows = rows_ref[...] if depth == 1 else rows_ref[pl.ds(0, senders, stride=depth), :]
    hot = received_hot(index_ref[...], states)
    packed = pack(whole(jnp.dot(split3(received_slots(rows)), hot, preferred_element_type=F32)))
    for i in range(out_ref.shape[0]):
        out_ref[i] = packed


def returned_rows(dev_ref, window_ref, index_ref):
    masked = rows16(dev_ref) * window16(window_ref)
    turned = index_ref[...].T.astype(jnp.int32)
    found = [pick(masked, turned[WIDTH * j + 12 : WIDTH * j + 13]) for j in range(8)]
    return jnp.concatenate(found, axis=0).T


def multiplier_of(part, source_ref, window_ref):
    window = window16(window_ref)
    return window * (rows16(source_ref) + unpack((part[0] + part[1]) + (part[2] + part[3])))


def second_kernel(
    parts_ref, index_ref, dev_ref, source_ref, relax_ref, window_ref, src_ref, live_ref, couple_ref, out_ref, flat_ref
):
    senders = index_ref.shape[0]
    out_ref[pl.ds(1, senders, stride=2), :] = returned_rows(dev_ref, window_ref, index_ref)
    relax = jnp.concatenate([relax_ref[...]] * 4, axis=0)
    moment = relax * multiplier_of(parts_ref, source_ref, window_ref)
    terms = scatter_terms(select(moment, src_ref[...]), live_ref[...], couple_ref[...])
    rows = to_places(slots_to_rows(terms, flat_ref))
    out_ref[pl.ds(0, senders, stride=2), :] = rows


def last_kernel(
    parts_ref, rows_ref, source_ref, relax_ref, window_ref, src_ref, live_ref, multiplier_ref, grad_ref, flat_ref
):
    owners = rows_ref.shape[0] // 2
    rows = from_places(rows_ref[pl.ds(1, owners, stride=2), :])
    for j in range(8):
        flat_ref[pl.ds(j, owners, stride=8), :] = rows[:, WIDTH * j : WIDTH * (j + 1)]
    fetched = flat_ref[...].T
    relax = jnp.concatenate([relax_ref[...]] * 4, axis=0)
    multiplier = multiplier_of(parts_ref, source_ref, window_ref)
    for d in range(3):
        multiplier_ref[d] = multiplier[4 * d : 4 * d + 4]
    picked = select(relax * multiplier, src_ref[...])
    total = None
    for d in range(3):
        far = fetched[4 * d : 4 * d + 4]
        term = repeat_rows(picked, 4 * d, 1, 4) * jnp.concatenate([far] * 4, axis=0)
        total = term if total is None else total + term
    grad_ref[...] = total * live_ref[...]


def call(kernel, out_shape, scratch, *operands, cost=None):
    return pl.pallas_call(
        kernel,
        out_shape=out_shape,
        in_specs=[pl.BlockSpec(memory_space=pltpu.VMEM)] * len(operands),
        scratch_shapes=scratch,
        compiler_params=pltpu.CompilerParams(vmem_limit_bytes=24 * MIB),
        cost_estimate=cost,
    )(*operands)


def exchange(rows):
    pools = lax.axis_size("pool")
    members = [(place + first_chip(pools)) % pools for place in range(pools)]
    members[:2] = members[1::-1]
    x = rows.reshape(pools, -1, 128)
    x = lax.all_to_all(x, "pool", 0, 0, axis_index_groups=[members], tiled=True)
    return x.reshape(rows.shape)


def share(part):
    groups = lax.axis_size("pb")
    members = [(place + groups // 2) % groups for place in range(groups)]
    return lax.all_to_all(part, "pb", 0, 0, axis_index_groups=[members], tiled=True)


def local(
    adjoint_source, deviation, relax_time, band_window, pair_src, pair_dst, bucket_fill, coupling
):
    states = band_window.shape[0]
    slots = pair_src.shape[0]
    pools = lax.axis_size("pool")
    window = band_window.reshape(1, states)
    src = pair_src.reshape(1, slots)
    dst = pair_dst.reshape(1, slots)
    sds = jax.ShapeDtypeStruct
    flat = pltpu.VMEM((slots, WIDTH), F32)
    partial = sds((lax.axis_size("pb"), 8, states * 3 // 2), F32)

    cost = pl.CostEstimate(flops=10**10, bytes_accessed=0, transcendentals=0)
    zero = call(zero_kernel, sds((8, 128), F32), [], cost=cost)
    sent, live = call(
        first_kernel, (sds((pools, 128), F32), sds((1, slots), F32)), [flat],
        zero, coupling, adjoint_source, relax_time, window, src, dst, bucket_fill,
    )
    index = exchange(sent)
    gather = functools.partial(gather_kernel, states=states)
    parts = share(call(gather, partial, [], index, index))
    sent = call(
        second_kernel, sds((2 * pools, 128), F32), [flat],
        parts, index, deviation, adjoint_source, relax_time, window, src, live, coupling,
    )
    rows = exchange(sent)
    parts = share(call(gather, partial, [], rows, index))
    return call(
        last_kernel, (sds(adjoint_source.shape, F32), sds(coupling.shape, F32)), [flat],
        parts, rows, adjoint_source, relax_time, window, src, live,
    )


def solution(mesh):
    in_specs = (
        P(None, None, "pool"),
        P(None, None, "pool"),
        P(None, "pool"),
        P("pool"),
        P(("pool", "pb")),
        P(("pool", "pb")),
        P(("pool", "pb"), None),
        P(None, ("pool", "pb")),
    )
    out_specs = (P(None, None, "pool"), P(None, ("pool", "pb")))
    return jax.shard_map(local, mesh=mesh, in_specs=in_specs, out_specs=out_specs, check_vma=False)
```

```python
import functools

import jax
import jax.numpy as jnp
from jax import lax
from jax.experimental import pallas as pl
from jax.experimental.pallas import tpu as pltpu
from jax.sharding import PartitionSpec as P

ITERS = 2
WIDTH = 16
F32 = jnp.float32
BF16 = jnp.bfloat16
MIB = 1024 * 1024


def split3(x):
    high = x.astype(BF16)
    rest = x - high.astype(F32)
    middle = rest.astype(BF16)
    low = (rest - middle.astype(F32)).astype(BF16)
    return jnp.concatenate([high, middle, low], axis=0)


def tiles_of(x):
    parts = split3(x)
    width = min(128, x.shape[1])
    return jnp.concatenate([parts[:, t : t + width] for t in range(0, x.shape[1], width)], axis=0)


def whole(parts):
    return parts[:16] + parts[16:32] + parts[32:48]


def select(x, index):
    width = min(128, x.shape[1])
    rows = lax.broadcasted_iota(jnp.int32, (width, index.shape[1]), 0)
    hot = jnp.where(rows == (index & (width - 1)), 1.0, 0.0).astype(BF16)
    found = jnp.dot(tiles_of(x), hot, preferred_element_type=F32)
    at = jnp.broadcast_to(index, (16, index.shape[1])) >> (width.bit_length() - 1)
    total = whole(found[:48])
    for tile in range(1, x.shape[1] // width):
        total = jnp.where(at == tile, whole(found[48 * tile : 48 * tile + 48]), total)
    return total


def pick(x, index):
    parts = []
    width = min(128, index.shape[1])
    for first in range(0, index.shape[1], width):
        at = jnp.broadcast_to(index[:, first : first + width], (x.shape[0], width))
        part = jnp.zeros(at.shape, F32)
        for tile in range(x.shape[1] // 128):
            columns = x[:, 128 * tile : 128 * (tile + 1)]
            found = jnp.take_along_axis(columns, at & 127, axis=1, mode="promise_in_bounds")
            part = jnp.where(at >> 7 == tile, found, part)
        parts.append(part)
    return jnp.concatenate(parts, axis=1)


def rows16(ref):
    return jnp.concatenate([ref[0], ref[1], ref[2], jnp.zeros_like(ref[0])], axis=0)


def window16(window_ref):
    rows = lax.broadcasted_iota(jnp.int32, (16, window_ref.shape[1]), 0)
    return ((window_ref[...] >> (rows & 3)) & 1).astype(F32)


def live_row(fill_ref, slots):
    owners = fill_ref.shape[1]
    capacity = slots // owners
    fill = jnp.broadcast_to(fill_ref[...].astype(F32), (8, owners))
    lane = lax.broadcasted_iota(jnp.int32, (8, owners), 1)
    place = (lane & (capacity - 1)).astype(F32)
    parts = []
    for first in range(0, owners, owners // capacity):
        filled = jnp.take_along_axis(fill, first + (lane >> (capacity.bit_length() - 1)), axis=1, mode="promise_in_bounds")
        parts.append(jnp.where(place < filled, 1.0, 0.0)[:1])
    return jnp.concatenate(parts, axis=1)


def repeat_rows(x, first, step, count):
    row = lax.broadcasted_iota(jnp.int32, (16, x.shape[1]), 0)
    out = jnp.broadcast_to(x[first : first + 1], row.shape)
    for i in range(1, count):
        out = jnp.where(row >= 4 * i, x[first + step * i : first + step * i + 1], out)
    return out


def scatter_terms(picked, live, couple):
    total = None
    for band in range(4):
        block = couple[4 * band : 4 * band + 4]
        block = jnp.concatenate([block, block, block, jnp.zeros_like(block)], axis=0)
        term = block * repeat_rows(picked, band, 4, 3)
        total = term if total is None else total + term
    return total * live


def slots_to_rows(x, flat_ref):
    owners = x.shape[1] // 8
    flat_ref[...] = x.T
    return jnp.concatenate([flat_ref[pl.ds(j, owners, stride=8), :] for j in range(8)], axis=1)


def first_chip(pools):
    return pools * 53 // 64


def to_places(rows):
    start = first_chip(rows.shape[0])
    return jnp.concatenate([rows[start + 1 : start + 2], rows[start : start + 1], rows[start + 2 :], rows[:start]], axis=0)


def from_places(rows):
    rest = rows.shape[0] - first_chip(rows.shape[0])
    return jnp.concatenate([rows[rest:], rows[1:2], rows[:1], rows[2:rest]], axis=0)


def pack(x):
    half = x.shape[1] // 2
    tail = jnp.concatenate([x[8:12, :half], x[8:12, half:]], axis=0)
    return jnp.concatenate([x[:8], tail], axis=1)


def unpack(x):
    whole = x.shape[1] * 2 // 3
    tail = jnp.concatenate([x[:4, whole:], x[4:, whole:]], axis=1)
    return jnp.concatenate([x[:8, :whole], jnp.concatenate([tail, jnp.zeros_like(tail)], axis=0)], axis=0)


def received_slots(rows):
    turned = rows.T
    return jnp.concatenate([turned[WIDTH * j : WIDTH * (j + 1)] for j in range(8)], axis=1)


def received_hot(rows, states):
    width = min(256, states)
    lane = lax.broadcasted_iota(jnp.int32, (rows.shape[0], width), 1).astype(F32).astype(BF16)
    blocks = []
    for j in range(8):
        column = rows[:, WIDTH * j + 12 : WIDTH * j + 13]
        parts = [
            jnp.where((column - first).astype(BF16) == lane, jnp.ones_like(lane), jnp.zeros_like(lane))
            for first in range(0, states, width)
        ]
        blocks.append(jnp.concatenate(parts, axis=1))
    return jnp.concatenate(blocks, axis=0)


def zero_kernel(out_ref):
    out_ref[...] = jnp.zeros_like(out_ref)


def first_kernel(
    zero_ref, couple_ref, source_ref, relax_ref, window_ref, src_ref, dst_ref, fill_ref, out_ref, live_ref, flat_ref
):
    live = live_row(fill_ref, src_ref.shape[1])
    live_ref[...] = live
    relax = jnp.concatenate([relax_ref[...]] * 4, axis=0)
    moment = rows16(source_ref) * window16(window_ref) * relax
    terms = scatter_terms(pick(moment, src_ref[...]), live, couple_ref[...])
    row = lax.broadcasted_iota(jnp.int32, terms.shape, 0)
    terms = jnp.where(row == 12, dst_ref[...].astype(F32) + zero_ref[:1, :1], terms)
    out_ref[...] = to_places(slots_to_rows(terms, flat_ref))


def gather_kernel(rows_ref, index_ref, out_ref, *, states):
    senders = index_ref.shape[0]
    depth = rows_ref.shape[0] // senders
    rows = rows_ref[...] if depth == 1 else rows_ref[pl.ds(0, senders, stride=depth), :]
    hot = received_hot(index_ref[...], states)
    packed = pack(whole(jnp.dot(split3(received_slots(rows)), hot, preferred_element_type=F32)))
    for i in range(out_ref.shape[0]):
        out_ref[i] = packed


def returned_rows(dev_ref, window_ref, index_ref):
    masked = rows16(dev_ref) * window16(window_ref)
    turned = index_ref[...].T.astype(jnp.int32)
    found = [pick(masked, turned[WIDTH * j + 12 : WIDTH * j + 13]) for j in range(8)]
    return jnp.concatenate(found, axis=0).T


def multiplier_of(part, source_ref, window_ref):
    window = window16(window_ref)
    return window * (rows16(source_ref) + unpack((part[0] + part[1]) + (part[2] + part[3])))


def second_kernel(
    parts_ref, index_ref, dev_ref, source_ref, relax_ref, window_ref, src_ref, live_ref, couple_ref, out_ref, flat_ref
):
    senders = index_ref.shape[0]
    out_ref[pl.ds(1, senders, stride=2), :] = returned_rows(dev_ref, window_ref, index_ref)
    relax = jnp.concatenate([relax_ref[...]] * 4, axis=0)
    moment = relax * multiplier_of(parts_ref, source_ref, window_ref)
    terms = scatter_terms(select(moment, src_ref[...]), live_ref[...], couple_ref[...])
    rows = to_places(slots_to_rows(terms, flat_ref))
    out_ref[pl.ds(0, senders, stride=2), :] = rows


def last_kernel(
    parts_ref, rows_ref, source_ref, relax_ref, window_ref, src_ref, live_ref, multiplier_ref, grad_ref, flat_ref
):
    owners = rows_ref.shape[0] // 2
    rows = from_places(rows_ref[pl.ds(1, owners, stride=2), :])
    for j in range(8):
        flat_ref[pl.ds(j, owners, stride=8), :] = rows[:, WIDTH * j : WIDTH * (j + 1)]
    fetched = flat_ref[...].T
    relax = jnp.concatenate([relax_ref[...]] * 4, axis=0)
    multiplier = multiplier_of(parts_ref, source_ref, window_ref)
    for d in range(3):
        multiplier_ref[d] = multiplier[4 * d : 4 * d + 4]
    picked = select(relax * multiplier, src_ref[...])
    total = None
    for d in range(3):
        far = fetched[4 * d : 4 * d + 4]
        term = repeat_rows(picked, 4 * d, 1, 4) * jnp.concatenate([far] * 4, axis=0)
        total = term if total is None else total + term
    grad_ref[...] = total * live_ref[...]


def call(kernel, out_shape, scratch, *operands, cost=None):
    return pl.pallas_call(
        kernel,
        out_shape=out_shape,
        in_specs=[pl.BlockSpec(memory_space=pltpu.VMEM)] * len(operands),
        scratch_shapes=scratch,
        compiler_params=pltpu.CompilerParams(vmem_limit_bytes=24 * MIB),
        cost_estimate=cost,
    )(*operands)


def exchange(rows):
    pools = lax.axis_size("pool")
    members = [(place + first_chip(pools)) % pools for place in range(pools)]
    members[:2] = members[1::-1]
    x = rows.reshape(pools, -1, 128)
    x = lax.all_to_all(x, "pool", 0, 0, axis_index_groups=[members], tiled=True)
    return x.reshape(rows.shape)


def share(part):
    groups = lax.axis_size("pb")
    members = [(place + groups // 2) % groups for place in range(groups)]
    return lax.all_to_all(part, "pb", 0, 0, axis_index_groups=[members], tiled=True)


def local(
    adjoint_source, deviation, relax_time, band_window, pair_src, pair_dst, bucket_fill, coupling
):
    states = band_window.shape[0]
    slots = pair_src.shape[0]
    pools = lax.axis_size("pool")
    window = band_window.reshape(1, states)
    src = pair_src.reshape(1, slots)
    dst = pair_dst.reshape(1, slots)
    sds = jax.ShapeDtypeStruct
    flat = pltpu.VMEM((slots, WIDTH), F32)
    partial = sds((lax.axis_size("pb"), 8, states * 3 // 2), F32)

    cost = pl.CostEstimate(flops=10**10, bytes_accessed=0, transcendentals=0)
    zero = call(zero_kernel, sds((8, 128), F32), [], cost=cost)
    sent, live = call(
        first_kernel, (sds((pools, 128), F32), sds((1, slots), F32)), [flat],
        zero, coupling, adjoint_source, relax_time, window, src, dst, bucket_fill,
    )
    index = exchange(sent)
    gather = functools.partial(gather_kernel, states=states)
    parts = share(call(gather, partial, [], index, index))
    sent = call(
        second_kernel, sds((2 * pools, 128), F32), [flat],
        parts, index, deviation, adjoint_source, relax_time, window, src, live, coupling,
    )
    rows = exchange(sent)
    parts = share(call(gather, partial, [], rows, index))
    return call(
        last_kernel, (sds(adjoint_source.shape, F32), sds(coupling.shape, F32)), [flat],
        parts, rows, adjoint_source, relax_time, window, src, live,
    )


def solution(mesh):
    in_specs = (
        P(None, None, "pool"),
        P(None, None, "pool"),
        P(None, "pool"),
        P("pool"),
        P(("pool", "pb")),
        P(("pool", "pb")),
        P(("pool", "pb"), None),
        P(None, ("pool", "pb")),
    )
    out_specs = (P(None, None, "pool"), P(None, ("pool", "pb")))
    return jax.shard_map(local, mesh=mesh, in_specs=in_specs, out_specs=out_specs, check_vma=False)
```
